32 devices in a mesh: dp: 2 (over y), expert: 16 (over z, x, core).
Axes of the slice: x: 2, y: 2, z: 4, core: 2. Of those that a mesh axis runs over, the one named last changes fastest.
Arguments:
- tokens: bfloat16 [2048, 7168], P('expert', 'dp'), may hold values from -6 to 6
- route_ids: int32 [2048, 8], P('expert'), may hold values from 0 to 15, all different within a row; in each aligned block of 128 rows (0 to 127, 128 to 255, ...) at most 80 rows name the same one
- route_weights: float32 [2048, 8], P('expert'), may hold values from 0.1 to 0.6
- swap_flags: int32 [16], replicated, may hold values from 0 to 1, as said below
- gate_weight: bfloat16 [16, 7168, 1024], P('expert', 'dp'), may hold values from -0.0625 to 0.0625
- up_weight: bfloat16 [16, 7168, 1024], P('expert', 'dp'), may hold values from -0.0625 to 0.0625
- down_weight: bfloat16 [16, 1024, 7168], P('expert', None, 'dp'), may hold values from -0.1875 to 0.1875
Outputs:
- mixed: bfloat16 [2048, 7168], P('expert', 'dp')
The draws below stay inside these ranges and needn't reach their ends.
Inputs may be any that keep to these rules, and one draw needn't show every extreme that they name: `route_ids`: each row names 8 different slots. In each aligned block of 128 rows (the rows of one device along `expert`) no slot is named by more than 80 rows, a bound that some block reaches. swap_flags[s] equals swap_flags[(s + 8) mod 16] for every slot s; swap_flags[0] and swap_flags[7] are 1 and swap_flags[1] is 0.
All inputs are finite; a program needn't handle non-finite values.
Results may differ from the reference program's by a relative error of at most 0.019.
Values may be sent and summed in bfloat16 or wider, within the bound.
A program may use at most 128 MiB of HBM per device.

```python
import math
import jax
import jax.numpy as jnp
import numpy as np
from jax import lax

D = 7168
H = 1024
K = 8
TOK_DEV = 128
EXPERTS = 16
TOKENS = 2048
CAP = 80
N_DP = 2


def draw_swap_flags(key, part):
    half_count = EXPERTS // 2
    raw_bits = jax.random.randint(jax.random.fold_in(key, 40503), (half_count,), 0, 2).astype(jnp.int32)
    paired_bits = raw_bits.at[0].set(1)
    paired_bits = paired_bits.at[1].set(0)
    paired_bits = paired_bits.at[half_count - 1].set(1)
    return jnp.concatenate([paired_bits, paired_bits]).astype(jnp.int32)


def block_scale(key, extent, split, least, largest):
    def one(dim, shards_of):
        steps = jax.random.uniform(jax.random.fold_in(jax.random.fold_in(key, 6), dim), (shards_of,), jnp.float32, least / len(split), largest / len(split))
        return jnp.repeat(jnp.exp(steps), extent[dim] // shards_of).reshape((-1,) + (1,) * (len(extent) - dim - 1))

    level = one(*split[0])
    for cut in split[1:]:
        level = level * one(*cut)
    return level


def deal_out(rng, own, number, rows, number_of, top, most, skew):
    order = jax.random.permutation(rng, number_of)
    packed, ordinary = portions_of(number_of, rows * top, most, skew, True), portions_of(number_of, rows * top, most, skew, False)
    places = jnp.arange(number_of)

    def named(tallies, offset_by):
        used = int((tallies > 0).sum())
        fixed = max(1, used // 4)
        moved = fixed + (places - fixed + offset_by * (used - fixed)) % max(1, number_of - fixed)
        return jnp.zeros((number_of,), jnp.int32).at[order[jnp.where(places < fixed, places, moved)]].set(jnp.asarray(tallies, jnp.int32))

    tallies = jnp.where(number % 4 == 0, named(packed, number // 4), named(ordinary, number - number // 4 - 1))
    mixed = jax.random.permutation(jax.random.fold_in(own, 3), number_of)
    giver, taker = mixed[0:number_of // 2 * 2:2], mixed[1:number_of // 2 * 2:2]
    margin = jnp.minimum(tallies[giver] - 1, most - tallies[taker]) // 2
    margin = jnp.where((giver == order[0]) | (taker == order[0]) | (tallies[taker] == 0), 0, jnp.maximum(margin, 0))
    moved = jax.random.randint(jax.random.fold_in(own, 4), (number_of // 2,), 0, 1 << 20) % (margin + 1)
    tallies = tallies.at[giver].add(-moved).at[taker].add(moved)
    labels = jnp.searchsorted(jnp.cumsum(tallies), jnp.arange(rows * top), side="right").astype(jnp.int32)
    table = labels.reshape(top, rows).T
    table = table[jax.random.permutation(jax.random.fold_in(own, 1), rows)]
    offset_by = jax.random.randint(jax.random.fold_in(own, 2), (rows, 1), 0, top)
    return jnp.take_along_axis(table, (jnp.arange(top)[None, :] + offset_by) % top, axis=1)


def portions_of(number_of, total, reach, skew, full):
    loads = [(1 << 20) // math.isqrt(rank ** skew) + 1 for rank in range(1, number_of + 1)]
    largest = reach if full else min(reach, max(-(-total // number_of), total * loads[0] // sum(loads)))
    least = 1 if total - largest >= number_of - 1 else 0
    counts, rest = [largest] + [least] * (number_of - 1), total - largest - least * (number_of - 1)
    while rest > 0:
        free = [i for i in range(1, number_of) if counts[i] < largest] or [i for i in range(1, number_of) if counts[i] < reach]
        mass, remaining = sum([loads[i] for i in free]), rest
        for i in free:
            addition = min(reach - counts[i], max(1, remaining * loads[i] // mass), rest)
            counts[i] = counts[i] + addition
            rest = rest - addition
    return np.array(counts)


def gaussian(key, extent, spread, most, cuts=(), kind=jnp.bfloat16):
    result = jax.random.normal(key, extent, jnp.float32) * spread
    if len(cuts) > 0:
        result = block_scale(key, extent, cuts, -0.22, 0.18) * result
    return jnp.clip(result, min=-most, max=most).astype(kind)


def setup_inputs(seed: int = 0) -> dict:
    key_of = jax.random.split(jax.random.key(seed), 8)
    tokens = gaussian(key_of[0], (TOKENS, D), 1.0, 6.0, ((0, 16), (1, 2)))
    route_ids_keys = jax.random.split(jax.random.fold_in(key_of[1], 1), TOKENS // TOK_DEV)
    route_ids_turns = jax.random.permutation(jax.random.fold_in(key_of[1], 3), TOKENS // TOK_DEV)
    route_ids = jax.vmap(lambda own, number: deal_out(jax.random.fold_in(key_of[1], 2), own, number, TOK_DEV, EXPERTS, K, CAP, 2))(route_ids_keys, route_ids_turns).reshape((TOKENS, K))
    route_weights = jnp.clip(0.1 + 0.5 * jax.random.uniform(key_of[2], (TOKENS, K), jnp.float32) ** block_scale(key_of[2], (TOKENS, K), ((0, 16),), -0.2, 0.2), 0.1, 0.6)
    swap_flags = draw_swap_flags(jax.random.fold_in(key_of[7], 71), 0)
    gate_weight = gaussian(key_of[4], (EXPERTS, D, H), D ** -0.5, 0.0625, ((0, 16), (1, 2)))
    up_weight = gaussian(key_of[5], (EXPERTS, D, H), D ** -0.5, 0.0625, ((0, 16), (1, 2)))
    down_weight = gaussian(key_of[6], (EXPERTS, H, D), H ** -0.5, 0.1875, ((0, 16), (2, 2)))
    return dict(tokens=tokens, route_ids=route_ids, route_weights=route_weights, swap_flags=swap_flags, gate_weight=gate_weight, up_weight=up_weight, down_weight=down_weight)


def rounded_sum(row_block, weight_block):
    quarter = D // N_DP
    total_sum = jnp.zeros((row_block.shape[0], weight_block.shape[1]), jnp.float32)
    for quarter_index in range(N_DP):
        column_start = quarter_index * quarter
        partial_term = jnp.dot(row_block[:, column_start:column_start + quarter], weight_block[column_start:column_start + quarter], preferred_element_type=jnp.float32).astype(jnp.bfloat16)
        total_sum = total_sum + lax.optimization_barrier(partial_term).astype(jnp.float32)
    return total_sum


def reference(tokens, route_ids, route_weights, swap_flags, gate_weight, up_weight, down_weight):
    slot_ids = jnp.arange(EXPERTS, dtype=jnp.int32)
    slot_source = jnp.where(swap_flags == 1, (slot_ids + EXPERTS // 2) % EXPERTS, slot_ids).astype(jnp.int32)
    flat_ids = route_ids.reshape(-1).astype(jnp.int32)
    entries = flat_ids.shape[0]
    sort_order = jnp.argsort(flat_ids, stable=True).astype(jnp.int32)
    slot_counts = jnp.sum((flat_ids[:, None] == slot_ids[None, :]).astype(jnp.int32), axis=0)
    slot_starts = (jnp.cumsum(slot_counts) - slot_counts).astype(jnp.int32)
    flat_weights = route_weights.reshape(-1)
    most_rows = EXPERTS * CAP

    def one_expert(expert_index, mixed_sum):
        offsets = jnp.arange(most_rows, dtype=jnp.int32)
        live_rows = offsets < slot_counts[expert_index]
        entry_ids = sort_order[jnp.minimum(slot_starts[expert_index] + offsets, entries - 1)]
        token_ids = (entry_ids // K).astype(jnp.int32)
        gathered = tokens[token_ids]
        row_block = jnp.where(live_rows[:, None], gathered, jnp.zeros_like(gathered))
        owner_slot = slot_source[expert_index]
        gate_sum = rounded_sum(row_block, gate_weight[owner_slot])
        up_sum = rounded_sum(row_block, up_weight[owner_slot])
        activated = (jax.nn.silu(gate_sum) * up_sum).astype(jnp.bfloat16)
        expert_out = jnp.dot(activated, down_weight[owner_slot], preferred_element_type=jnp.float32).astype(jnp.bfloat16)
        row_weight = jnp.where(live_rows, flat_weights[entry_ids], jnp.zeros_like(flat_weights[entry_ids]))
        return mixed_sum.at[token_ids].add(row_weight[:, None] * expert_out.astype(jnp.float32))

    mixed_sum = lax.fori_loop(0, EXPERTS, one_expert, jnp.zeros((tokens.shape[0], D), jnp.float32))
    return mixed_sum.astype(jnp.bfloat16)
```

```python
import jax
import jax.numpy as jnp
from jax import lax
from jax.sharding import PartitionSpec as P


def per_device(tokens, route_ids, route_weights, swap_flags, gate_weight, up_weight, down_weight):
    experts = lax.axis_size("expert")
    tok_rows, quarter = tokens.shape
    choices_per = route_ids.shape[1]
    hidden = gate_weight.shape[2]
    capacity = max(2, min(tok_rows, 5 * tok_rows * choices_per // (4 * experts)))
    me = lax.axis_index("expert")
    my_slot = jnp.where(swap_flags[me] == 1, (me + experts // 2) % experts, me)

    slots = jnp.arange(experts, dtype=jnp.int32)
    dense = jnp.sum(
        jnp.where(route_ids[:, :, None] == slots[None, None, :], route_weights[:, :, None], 0.0), axis=1
    )
    all_dense = lax.all_gather(dense, "expert", axis=0, tiled=False)
    all_tokens = lax.all_gather(tokens, "expert", axis=0, tiled=False)
    mine = jnp.sum(jnp.where(slots[None, None, :] == my_slot, all_dense, 0.0), axis=2)
    chosen = mine > 0.0
    rank = jnp.cumsum(chosen.astype(jnp.int32), axis=1) - 1
    places = jnp.arange(capacity, dtype=jnp.int32)
    pick = ((rank[:, None, :] == places[None, :, None]) & chosen[:, None, :]).astype(jnp.bfloat16)

    rows = jnp.einsum("bct,btd->bcd", pick, all_tokens, preferred_element_type=jnp.bfloat16)
    rows = rows.reshape(experts * capacity, quarter)
    gate_term = jnp.dot(rows, gate_weight[0], preferred_element_type=jnp.float32)
    up_term = jnp.dot(rows, up_weight[0], preferred_element_type=jnp.float32)
    summed = lax.psum_scatter(
        jnp.concatenate([gate_term, up_term], axis=1).astype(jnp.bfloat16),
        "dp",
        scatter_dimension=0,
        tiled=True,
    ).astype(jnp.float32)
    activated = (jax.nn.silu(summed[:, :hidden]) * summed[:, hidden:]).astype(jnp.bfloat16)
    results = jnp.dot(
        lax.all_gather(activated, "dp", axis=0, tiled=True),
        down_weight[0],
        preferred_element_type=jnp.float32,
    ).astype(jnp.bfloat16)
    results = results.reshape(experts, capacity, quarter)
    spread = jnp.einsum("bct,bcd->btd", pick, results, preferred_element_type=jnp.float32)
    weighted = (mine[:, :, None] * spread).astype(jnp.bfloat16)
    return lax.psum_scatter(weighted, "expert", scatter_dimension=0, tiled=False)


def solution(mesh):
    in_specs = (
        P("expert", "dp"),
        P("expert", None),
        P("expert", None),
        P(),
        P("expert", "dp", None),
        P("expert", "dp", None),
        P("expert", None, "dp"),
    )
    out_specs = P("expert", "dp")
    return jax.shard_map(
        per_device, mesh=mesh, in_specs=in_specs, out_specs=out_specs, check_vma=False
    )
```

```python
import functools

import jax
import jax.numpy as jnp
from jax import lax
from jax.experimental import pallas as pl
from jax.experimental.pallas import tpu as pltpu
from jax.sharding import PartitionSpec as P

BF16 = jnp.bfloat16
F32 = jnp.float32
LINE = 4
GROUPS = 8
VMEM_BYTES = 63 * 1024 * 1024


def fused_kernel(
    cap, served_ref, tokens_ref, gate_ref, up_ref, down_ref, out_ref,
    tok, wgu, wd, rows, dense, gu_send, gu_own, gu_recv, act_own, act_recv, rc, rx, rz,
    load_sem, meta_ss, meta_rs,
    zu_ss, zd_ss, z_rs, x_ss, x_rs, c_ss, c_rs,
    g_ss, g_rs, a_ss, a_rs,
    pc_ss, pc_rs, px_ss, px_rs, pz_ss, pz_rs,
):
    d = lax.axis_index("dp")
    e = lax.axis_index("expert")
    experts = LINE * 4
    width = tok.shape[2]
    hidden = wd.shape[0]
    half = hidden // 2
    z = e // 4
    x = (e // 2) % 2
    c = e % 2
    up_dev, down_dev = e + 4, e - 4
    x_dev = z * 4 + (1 - x) * 2 + c
    c_dev = z * 4 + x * 2 + (1 - c)
    low = z < 2
    m = jnp.where(low, z, LINE - 1 - z)
    mid = m == 1

    def order(i):
        o = jnp.where(i == 0, m, jnp.where(i - 1 < m, i - 1, i))
        return jnp.where(low, o, LINE - 1 - o)

    def group(i):
        zz = order(i // 2)
        xx = jnp.where(i % 2 == 0, x, 1 - x)
        return zz, xx

    def block(zz, xx, cc):
        return zz * 4 + xx * 2 + cc

    def remote(src, dst, ss, rs, dev):
        return pltpu.make_async_remote_copy(
            src_ref=src, dst_ref=dst, send_sem=ss, recv_sem=rs,
            device_id=(d, dev), device_id_type=pl.DeviceIdType.MESH,
        )

    def to_partner(src, dst, ss, rs):
        return pltpu.make_async_remote_copy(
            src_ref=src, dst_ref=dst, send_sem=ss, recv_sem=rs,
            device_id=(1 - d, e), device_id_type=pl.DeviceIdType.MESH,
        )

    loads = [
        pltpu.make_async_copy(tokens_ref, tok.at[e], load_sem.at[0]),
        pltpu.make_async_copy(gate_ref, wgu.at[:, pl.ds(0, hidden)], load_sem.at[1]),
        pltpu.make_async_copy(up_ref, wgu.at[:, pl.ds(hidden, hidden)], load_sem.at[2]),
        pltpu.make_async_copy(down_ref, wd, load_sem.at[3]),
        pltpu.make_async_copy(served_ref, dense.at[e], load_sem.at[4]),
    ]
    for load in loads:
        load.start()

    barrier = pltpu.get_barrier_semaphore()

    @pl.loop(1, experts)
    def _(k):
        pl.semaphore_signal(
            barrier, inc=1, device_id=(d, (e + k) % experts), device_id_type=pl.DeviceIdType.MESH
        )

    pl.semaphore_signal(barrier, inc=1, device_id=(1 - d, e), device_id_type=pl.DeviceIdType.MESH)
    pl.semaphore_wait(barrier, experts)

    def z_up(zz):
        b = tok.at[block(zz, x, c)]
        return remote(b, b, zu_ss.at[zz], z_rs.at[zz], up_dev)

    def z_down(zz):
        b = tok.at[block(zz, x, c)]
        return remote(b, b, zd_ss.at[zz], z_rs.at[zz], down_dev)

    def x_copy(zz, xx):
        b = tok.at[block(zz, xx, c)]
        return remote(b, b, x_ss.at[zz], x_rs.at[zz], x_dev)

    def c_copy(zz, xx, cc):
        b = tok.at[block(zz, xx, cc)]
        return remote(b, b, c_ss.at[zz * 2 + xx], c_rs.at[zz * 2 + xx], c_dev)

    def sends_up(zz):
        return jnp.logical_and(zz <= z, z < LINE - 1)

    def sends_down(zz):
        return jnp.logical_and(zz >= z, z > 0)

    def spread_column(zz):
        @pl.when(sends_up(zz))
        def _():
            z_up(zz).start()

        @pl.when(sends_down(zz))
        def _():
            z_down(zz).start()

        x_copy(zz, x).start()
        c_copy(zz, x, c).start()

    def take_column(zz):
        b = tok.at[block(zz, x, c)]
        remote(b, b, zu_ss.at[zz], z_rs.at[zz], c_dev).wait_recv()
        spread_column(zz)

    loads[0].wait()
    spread_column(z)
    loads[4].wait()

    def meta_copy(src, dst_dev):
        return remote(dense.at[src], dense.at[src], meta_ss.at[dst_dev], meta_rs.at[src], dst_dev)

    @pl.loop(1, experts)
    def _(k):
        meta_copy(e, (e + k) % experts).start()

    @pl.loop(1, experts)
    def _(k):
        meta_copy((e + k) % experts, (e + k) % experts).wait_recv()

    for load in loads[1:4]:
        load.wait()

    tri = jnp.where(
        lax.broadcasted_iota(jnp.int32, (128, 128), 0) <= lax.broadcasted_iota(jnp.int32, (128, 128), 1), 1.0, 0.0
    ).astype(BF16)

    def keys(b):
        w = dense[b, pl.ds(e, 1), :]
        chosen = w > 0.0
        ones = jnp.broadcast_to(jnp.where(chosen, 1.0, 0.0), (16, 128)).astype(BF16)
        rank = jnp.dot(ones, tri, preferred_element_type=F32)[0:1]
        return w, jnp.where(chosen, rank - 1.0, -1000.0)

    def gate_up(i):
        zz, xx = group(i)
        for k in range(2):
            b = block(zz, xx, c if k == 0 else 1 - c)
            _, key = keys(b)
            place = lax.broadcasted_iota(jnp.int32, (cap, 128), 0).astype(F32)
            pick = jnp.where(place == jnp.broadcast_to(key, (cap, 128)), 1.0, 0.0).astype(BF16)

            @pl.loop(0, width // 512)
            def _(t):
                cols = pl.ds(pl.multiple_of(t * 512, 512), 512)
                rows[pl.ds(k * cap, cap), cols] = jnp.dot(
                    pick, tok[b, :, cols], preferred_element_type=F32
                ).astype(BF16)

        slot = i % 2

        @pl.when(i >= 2)
        def _():
            gu_copy(i - 2).wait_send()

        def tile(t, which):
            at = pl.multiple_of((t // 2) * hidden + which * half + (t % 2) * 256, 256)
            return jnp.dot(rows[...], wgu[:, pl.ds(at, 256)], preferred_element_type=F32).astype(BF16)

        @pl.loop(0, 4)
        def _(t):
            gu_send[slot, :, pl.ds(pl.multiple_of(t * 256, 256), 256)] = tile(t, 1 - d)

        gu_copy(i).start()

        @pl.loop(0, 4)
        def _(t):
            gu_own[slot, :, pl.ds(pl.multiple_of(t * 256, 256), 256)] = tile(t, d)

    def gu_copy(i):
        return to_partner(gu_send.at[i % 2], gu_recv.at[i], g_ss.at[i], g_rs.at[i])

    def act_copy(i):
        return to_partner(act_own.at[i], act_recv.at[i], a_ss.at[i], a_rs.at[i])

    def activate(i):
        gu_copy(i).wait_recv()
        slot = i % 2

        @pl.loop(0, half // 128)
        def _(t):
            cg = pl.ds(pl.multiple_of(t * 128, 128), 128)
            cu = pl.ds(pl.multiple_of(half + t * 128, 128), 128)
            g = gu_own[slot, :, cg].astype(F32) + gu_recv[i, :, cg].astype(F32)
            u = gu_own[slot, :, cu].astype(F32) + gu_recv[i, :, cu].astype(F32)
            act_own[i, :, cg] = (g / (1.0 + jnp.exp(-g)) * u).astype(BF16)

        act_copy(i).start()

    def pc_copy(i):
        zz, xx = group(i)
        at = zz * 2 + xx
        return remote(tok.at[block(zz, xx, 1 - c)], rc.at[at], pc_ss.at[at], pc_rs.at[at], c_dev)

    def px_copy(zz):
        return remote(tok.at[block(zz, 1 - x, c)], rx.at[zz], px_ss.at[zz], px_rs.at[zz], x_dev)

    def down(i):
        zz, xx = group(i)
        act_copy(i).wait_recv()
        c_copy(zz, xx, c).wait_send()

        @pl.when(i % 2 == 0)
        def _():
            x_copy(zz, x).wait_send()

            @pl.when(sends_up(zz))
            def _():
                z_up(zz).wait_send()

            @pl.when(sends_down(zz))
            def _():
                z_down(zz).wait_send()

        for k in (1, 0):
            b = block(zz, xx, c if k == 0 else 1 - c)
            w, key = keys(b)
            place = lax.broadcasted_iota(jnp.int32, (128, 128), 0).astype(F32)
            key = key + float(k * (128 - cap))
            put = jnp.transpose(jnp.where(place == jnp.broadcast_to(key, (128, 128)), 1.0, 0.0)).astype(BF16)
            col = jnp.transpose(jnp.broadcast_to(w, (128, 128)))[:, 0:1]
            lo = k * (2 * cap - 128)

            @pl.loop(0, width // 512)
            def _(t):
                cols = pl.ds(pl.multiple_of(t * 512, 512), 512)
                mine = act_own[i, pl.ds(lo, 128), :]
                theirs = act_recv[i, pl.ds(lo, 128), :]
                o = jnp.dot(mine, wd[pl.ds(pl.multiple_of(d * half, half), half), cols], preferred_element_type=F32)
                o = o + jnp.dot(
                    theirs, wd[pl.ds(pl.multiple_of((1 - d) * half, half), half), cols], preferred_element_type=F32
                )
                s = jnp.dot(put, o.astype(BF16), preferred_element_type=F32)
                tok[b, :, cols] = (s * col).astype(BF16)

            if k == 1:
                pc_copy(i).start()

    def add_into(b, other, at):
        @pl.loop(0, width // 512)
        def _(t):
            cols = pl.ds(pl.multiple_of(t * 512, 512), 512)
            tok[b, :, cols] = (tok[b, :, cols].astype(F32) + other[at, :, cols].astype(F32)).astype(BF16)

    def reduce_core(i):
        zz, xx = group(i)
        pc_copy(i).wait_recv()
        add_into(block(zz, xx, c), rc, zz * 2 + xx)

        @pl.when(i % 2 == 1)
        def _():
            px_copy(zz).start()

    def pz_up(zz):
        return remote(tok.at[block(zz, x, c)], rz.at[zz], pz_ss.at[zz], pz_rs.at[zz], up_dev)

    def pz_down(zz):
        at = jnp.where(zz == z - 1, LINE, zz)
        return remote(tok.at[block(zz, x, c)], rz.at[at], pz_ss.at[zz], pz_rs.at[at], down_dev)

    def send_on(zz):
        @pl.when(zz > z)
        def _():
            pz_up(zz).start()

        @pl.when(zz < z)
        def _():
            pz_down(zz).start()

    def rz_wait(at):
        remote(rz.at[at], rz.at[at], pz_ss.at[0], pz_rs.at[at], c_dev).wait_recv()

    def reduce_x(zi):
        zz = order(zi)
        px_copy(zz).wait_recv()
        add_into(block(zz, x, c), rx, zz)

        @pl.when(jnp.logical_and(zi > 0, jnp.logical_not(mid)))
        def _():
            send_on(zz)

    @pl.loop(0, GROUPS + 4)
    def _(i):
        @pl.when(i < GROUPS)
        def _():
            zz, xx = group(i)

            @pl.when(i % 2 == 0)
            def _():
                @pl.when(jnp.logical_and(i > 0, jnp.logical_not(jnp.logical_and(mid, i == 4))))
                def _():
                    take_column(zz)

                @pl.when(jnp.logical_and(mid, i == 2))
                def _():
                    take_column(order(2))

            @pl.when(i % 2 == 1)
            def _():
                x_copy(zz, xx).wait_recv()
                c_copy(zz, xx, c).start()

            c_copy(zz, xx, 1 - c).wait_recv()

        @pl.when(jnp.logical_and(i >= 1, i < GROUPS + 1))
        def _():
            activate(i - 1)

        @pl.when(i < GROUPS)
        def _():
            gate_up(i)

        @pl.when(jnp.logical_and(i >= 2, i < GROUPS + 2))
        def _():
            down(i - 2)

        @pl.when(jnp.logical_and(i >= 3, i < GROUPS + 3))
        def _():
            reduce_core(i - 3)

        @pl.when(jnp.logical_and(i >= 5, i % 2 == 1))
        def _():
            reduce_x((i - 5) // 2)

    @pl.when(mid)
    def _():
        @pl.loop(0, 3)
        def _(k):
            zz = order(jnp.where(k == 2, 1, k + 2))
            rz_wait(zz)
            add_into(block(zz, x, c), rz, zz)
            send_on(zz)

    @pl.when(z > 0)
    def _():
        rz_wait(z)

    @pl.when(z < LINE - 1)
    def _():
        rz_wait(LINE)

    @pl.loop(0, width // 512)
    def _(t):
        cols = pl.ds(pl.multiple_of(t * 512, 512), 512)
        own = tok[e, :, cols].astype(F32)
        below = jnp.where(z > 0, rz[z, :, cols].astype(F32), 0.0)
        above = jnp.where(z < LINE - 1, rz[LINE, :, cols].astype(F32), 0.0)
        out_ref[:, cols] = (own + below + above).astype(BF16)

    @pl.loop(1, experts)
    def _(k):
        meta_copy(e, (e + k) % experts).wait_send()

    gu_copy(GROUPS - 2).wait_send()
    gu_copy(GROUPS - 1).wait_send()

    @pl.loop(0, GROUPS)
    def _(i):
        act_copy(i).wait_send()
        pc_copy(i).wait_send()

    @pl.loop(0, LINE)
    def _(zz):
        px_copy(zz).wait_send()

        @pl.when(zz > z)
        def _():
            pz_up(zz).wait_send()

        @pl.when(zz < z)
        def _():
            pz_down(zz).wait_send()


def fused(tokens, route_ids, route_weights, swap_flags, gate_weight, up_weight, down_weight):
    experts = lax.axis_size("expert")
    tok_rows, width = tokens.shape
    hidden = gate_weight.shape[2]
    cap = 5 * tok_rows * route_ids.shape[1] // (4 * experts)
    slots = jnp.arange(experts, dtype=jnp.int32)
    source = jnp.where(swap_flags == 1, (slots + experts // 2) % experts, slots)
    hit = route_ids[None, :, :] == source[:, None, None]
    served = jnp.sum(jnp.where(hit, route_weights[None], 0.0), axis=2)
    block = (tok_rows, width)
    dma = pltpu.SemaphoreType.DMA
    return pl.pallas_call(
        functools.partial(fused_kernel, cap),
        out_shape=jax.ShapeDtypeStruct(block, BF16),
        in_specs=[pl.BlockSpec(memory_space=pl.ANY)] * 5,
        out_specs=pl.BlockSpec(memory_space=pltpu.VMEM),
        scratch_shapes=[
            pltpu.VMEM((experts,) + block, BF16),
            pltpu.VMEM((width, 2 * hidden), BF16),
            pltpu.VMEM((hidden, width), BF16),
            pltpu.VMEM((2 * cap, width), BF16),
            pltpu.VMEM((experts, experts, tok_rows), F32),
            pltpu.VMEM((2, 2 * cap, hidden), BF16),
            pltpu.VMEM((2, 2 * cap, hidden), BF16),
            pltpu.VMEM((GROUPS, 2 * cap, hidden), BF16),
            pltpu.VMEM((GROUPS, 2 * cap, hidden // 2), BF16),
            pltpu.VMEM((GROUPS, 2 * cap, hidden // 2), BF16),
            pltpu.VMEM((GROUPS,) + block, BF16),
            pltpu.VMEM((LINE,) + block, BF16),
            pltpu.VMEM((LINE + 1,) + block, BF16),
            dma((5,)), dma((experts,)), dma((experts,)),
            dma((LINE,)), dma((LINE,)), dma((LINE,)), dma((LINE,)), dma((LINE,)), dma((GROUPS,)), dma((GROUPS,)),
            dma((GROUPS,)), dma((GROUPS,)), dma((GROUPS,)), dma((GROUPS,)),
            dma((GROUPS,)), dma((GROUPS,)), dma((LINE,)), dma((LINE,)), dma((LINE,)), dma((LINE + 1,)),
        ],
        compiler_params=pltpu.CompilerParams(
            collective_id=0, has_side_effects=True, vmem_limit_bytes=VMEM_BYTES
        ),
    )(served, tokens, gate_weight[0], up_weight[0], down_weight[0])


def per_device(tokens, route_ids, route_weights, swap_flags, gate_weight, up_weight, down_weight):
    experts = lax.axis_size("expert")
    tok_rows, quarter = tokens.shape
    choices_per = route_ids.shape[1]
    hidden = gate_weight.shape[2]
    capacity = max(2, min(tok_rows, 5 * tok_rows * choices_per // (4 * experts)))
    me = lax.axis_index("expert")
    my_slot = jnp.where(swap_flags[me] == 1, (me + experts // 2) % experts, me)

    slots = jnp.arange(experts, dtype=jnp.int32)
    dense = jnp.sum(
        jnp.where(route_ids[:, :, None] == slots[None, None, :], route_weights[:, :, None], 0.0), axis=1
    )
    all_dense = lax.all_gather(dense, "expert", axis=0, tiled=False)
    all_tokens = lax.all_gather(tokens, "expert", axis=0, tiled=False)
    mine = jnp.sum(jnp.where(slots[None, None, :] == my_slot, all_dense, 0.0), axis=2)
    chosen = mine > 0.0
    rank = jnp.cumsum(chosen.astype(jnp.int32), axis=1) - 1
    places = jnp.arange(capacity, dtype=jnp.int32)
    pick = ((rank[:, None, :] == places[None, :, None]) & chosen[:, None, :]).astype(jnp.bfloat16)

    rows = jnp.einsum("bct,btd->bcd", pick, all_tokens, preferred_element_type=jnp.bfloat16)
    rows = rows.reshape(experts * capacity, quarter)
    gate_term = jnp.dot(rows, gate_weight[0], preferred_element_type=jnp.float32)
    up_term = jnp.dot(rows, up_weight[0], preferred_element_type=jnp.float32)
    summed = lax.psum_scatter(
        jnp.concatenate([gate_term, up_term], axis=1).astype(jnp.bfloat16),
        "dp",
        scatter_dimension=0,
        tiled=True,
    ).astype(jnp.float32)
    activated = (jax.nn.silu(summed[:, :hidden]) * summed[:, hidden:]).astype(jnp.bfloat16)
    results = jnp.dot(
        lax.all_gather(activated, "dp", axis=0, tiled=True),
        down_weight[0],
        preferred_element_type=jnp.float32,
    ).astype(jnp.bfloat16)
    results = results.reshape(experts, capacity, quarter)
    spread = jnp.einsum("bct,bcd->btd", pick, results, preferred_element_type=jnp.float32)
    weighted = (mine[:, :, None] * spread).astype(jnp.bfloat16)
    return lax.psum_scatter(weighted, "expert", scatter_dimension=0, tiled=False)


def solution(mesh):
    fits = mesh.shape["expert"] == 4 * LINE and mesh.shape["dp"] == 2
    in_specs = (
        P("expert", "dp"),
        P("expert", None),
        P("expert", None),
        P(),
        P("expert", "dp", None),
        P("expert", "dp", None),
        P("expert", None, "dp"),
    )
    out_specs = P("expert", "dp")
    return jax.shard_map(
        fused if fits else per_device, mesh=mesh, in_specs=in_specs, out_specs=out_specs, check_vma=False
    )
```

```python
import functools

import jax
import jax.numpy as jnp
from jax import lax
from jax.experimental import pallas as pl
from jax.experimental.pallas import tpu as pltpu
from jax.sharding import PartitionSpec as P

BF16 = jnp.bfloat16
F32 = jnp.float32
LINE = 4
PIECES = 4
GROUPS = 8
VMEM_BYTES = 63 * 1024 * 1024


def fused_kernel(
    cap, served_ref, tokens_ref, gate_ref, up_ref, down_ref, out_ref,
    tok, wgu, wd, rows, dense, gu_send, gu_own, gu_recv, act_own, act_recv, rc, rx, rz,
    load_sem, meta_ss, meta_rs,
    zu_ss, zd_ss, z_rs, x_ss, x_rs, c_ss, c_rs,
    g_ss, g_rs, a_ss, a_rs,
    pc_ss, pc_rs, px_ss, px_rs, pz_ss, pz_rs,
):
    d = lax.axis_index("dp")
    e = lax.axis_index("expert")
    experts = LINE * 4
    width = tok.shape[2]
    hidden = wd.shape[0]
    half = hidden // 2
    z = e // 4
    x = (e // 2) % 2
    c = e % 2
    up_dev, down_dev = e + 4, e - 4
    x_dev = z * 4 + (1 - x) * 2 + c
    c_dev = z * 4 + x * 2 + (1 - c)
    low = z < 2
    m = jnp.where(low, z, LINE - 1 - z)
    mid = m == 1

    def order(i):
        o = jnp.where(i == 0, m, jnp.where(i - 1 < m, i - 1, i))
        return jnp.where(low, o, LINE - 1 - o)

    def group(i):
        zz = order(i // 2)
        xx = jnp.where(i % 2 == 0, x, 1 - x)
        return zz, xx

    def block(zz, xx, cc):
        return zz * 4 + xx * 2 + cc

    def remote(src, dst, ss, rs, dev):
        return pltpu.make_async_remote_copy(
            src_ref=src, dst_ref=dst, send_sem=ss, recv_sem=rs,
            device_id=(d, dev), device_id_type=pl.DeviceIdType.MESH,
        )

    def to_partner(src, dst, ss, rs):
        return pltpu.make_async_remote_copy(
            src_ref=src, dst_ref=dst, send_sem=ss, recv_sem=rs,
            device_id=(1 - d, e), device_id_type=pl.DeviceIdType.MESH,
        )

    loads = [
        pltpu.make_async_copy(tokens_ref, tok.at[e], load_sem.at[0]),
        pltpu.make_async_copy(gate_ref, wgu.at[:, pl.ds(0, hidden)], load_sem.at[1]),
        pltpu.make_async_copy(up_ref, wgu.at[:, pl.ds(hidden, hidden)], load_sem.at[2]),
        pltpu.make_async_copy(down_ref, wd, load_sem.at[3]),
        pltpu.make_async_copy(served_ref, dense.at[e], load_sem.at[4]),
    ]
    for load in loads:
        load.start()

    barrier = pltpu.get_barrier_semaphore()

    @pl.loop(1, experts)
    def _(k):
        pl.semaphore_signal(
            barrier, inc=1, device_id=(d, (e + k) % experts), device_id_type=pl.DeviceIdType.MESH
        )

    pl.semaphore_signal(barrier, inc=1, device_id=(1 - d, e), device_id_type=pl.DeviceIdType.MESH)
    pl.semaphore_wait(barrier, experts)

    def z_up(zz):
        b = tok.at[block(zz, x, c)]
        return remote(b, b, zu_ss.at[zz], z_rs.at[zz], up_dev)

    def z_down(zz):
        b = tok.at[block(zz, x, c)]
        return remote(b, b, zd_ss.at[zz], z_rs.at[zz], down_dev)

    def x_copy(zz, xx):
        b = tok.at[block(zz, xx, c)]
        return remote(b, b, x_ss.at[zz], x_rs.at[zz], x_dev)

    def c_copy(zz, xx, cc):
        b = tok.at[block(zz, xx, cc)]
        return remote(b, b, c_ss.at[zz * 2 + xx], c_rs.at[zz * 2 + xx], c_dev)

    def sends_up(zz):
        return jnp.logical_and(zz <= z, z < LINE - 1)

    def sends_down(zz):
        return jnp.logical_and(zz >= z, z > 0)

    def spread_column(zz):
        @pl.when(sends_up(zz))
        def _():
            z_up(zz).start()

        @pl.when(sends_down(zz))
        def _():
            z_down(zz).start()

        x_copy(zz, x).start()
        c_copy(zz, x, c).start()

    def take_column(zz):
        b = tok.at[block(zz, x, c)]
        remote(b, b, zu_ss.at[zz], z_rs.at[zz], c_dev).wait_recv()
        spread_column(zz)

    loads[0].wait()
    spread_column(z)
    loads[4].wait()

    def meta_copy(src, dst_dev):
        return remote(dense.at[src], dense.at[src], meta_ss.at[dst_dev], meta_rs.at[src], dst_dev)

    @pl.loop(1, experts)
    def _(k):
        meta_copy(e, (e + k) % experts).start()

    @pl.loop(1, experts)
    def _(k):
        meta_copy((e + k) % experts, (e + k) % experts).wait_recv()

    for load in loads[1:4]:
        load.wait()

    tri = jnp.where(
        lax.broadcasted_iota(jnp.int32, (128, 128), 0) <= lax.broadcasted_iota(jnp.int32, (128, 128), 1), 1.0, 0.0
    ).astype(BF16)

    def keys(b):
        w = dense[b, pl.ds(e, 1), :]
        chosen = w > 0.0
        ones = jnp.broadcast_to(jnp.where(chosen, 1.0, 0.0), (16, 128)).astype(BF16)
        rank = jnp.dot(ones, tri, preferred_element_type=F32)[0:1]
        return w, jnp.where(chosen, rank - 1.0, -1000.0)

    def gate_up(i):
        zz, xx = group(i)
        for k in range(2):
            b = block(zz, xx, c if k == 0 else 1 - c)
            _, key = keys(b)
            place = lax.broadcasted_iota(jnp.int32, (cap, 128), 0).astype(F32)
            pick = jnp.where(place == jnp.broadcast_to(key, (cap, 128)), 1.0, 0.0).astype(BF16)

            @pl.loop(0, width // 512)
            def _(t):
                cols = pl.ds(pl.multiple_of(t * 512, 512), 512)
                rows[pl.ds(k * cap, cap), cols] = jnp.dot(
                    pick, tok[b, :, cols], preferred_element_type=F32
                ).astype(BF16)

        slot = i % 2

        @pl.when(i >= 2)
        def _():
            gu_copy(i - 2).wait_send()

        def tile(t, which):
            at = pl.multiple_of((t // 2) * hidden + which * half + (t % 2) * 256, 256)
            return jnp.dot(rows[...], wgu[:, pl.ds(at, 256)], preferred_element_type=F32).astype(BF16)

        @pl.loop(0, 4)
        def _(t):
            gu_send[slot, :, pl.ds(pl.multiple_of(t * 256, 256), 256)] = tile(t, 1 - d)

        gu_copy(i).start()

        @pl.loop(0, 4)
        def _(t):
            gu_own[slot, :, pl.ds(pl.multiple_of(t * 256, 256), 256)] = tile(t, d)

    def gu_copy(i):
        return to_partner(gu_send.at[i % 2], gu_recv.at[i], g_ss.at[i], g_rs.at[i])

    def act_copy(i):
        return to_partner(act_own.at[i], act_recv.at[i], a_ss.at[i], a_rs.at[i])

    def activate(i):
        gu_copy(i).wait_recv()
        slot = i % 2

        @pl.loop(0, half // 128)
        def _(t):
            cg = pl.ds(pl.multiple_of(t * 128, 128), 128)
            cu = pl.ds(pl.multiple_of(half + t * 128, 128), 128)
            g = gu_own[slot, :, cg].astype(F32) + gu_recv[i, :, cg].astype(F32)
            u = gu_own[slot, :, cu].astype(F32) + gu_recv[i, :, cu].astype(F32)
            act_own[i, :, cg] = (g / (1.0 + jnp.exp(-g)) * u).astype(BF16)

        act_copy(i).start()

    def pc_copy(i):
        zz, xx = group(i)
        at = zz * 2 + xx
        return remote(tok.at[block(zz, xx, 1 - c)], rc.at[at], pc_ss.at[at], pc_rs.at[at], c_dev)

    piece = width // PIECES

    def part(t):
        return pl.ds(pl.multiple_of(t * piece, 128), piece)

    def px_copy(zz, t):
        return remote(
            tok.at[block(zz, 1 - x, c), :, part(t)], rx.at[zz, :, part(t)], px_ss.at[zz, t], px_rs.at[zz, t], x_dev
        )

    def px_start(zz):
        @pl.loop(0, PIECES)
        def _(t):
            px_copy(zz, t).start()

    def down(i):
        zz, xx = group(i)
        act_copy(i).wait_recv()
        c_copy(zz, xx, c).wait_send()

        @pl.when(i % 2 == 0)
        def _():
            x_copy(zz, x).wait_send()

            @pl.when(sends_up(zz))
            def _():
                z_up(zz).wait_send()

            @pl.when(sends_down(zz))
            def _():
                z_down(zz).wait_send()

        puts = []
        for k in range(2):
            b = block(zz, xx, c if k == 0 else 1 - c)
            w, key = keys(b)
            place = lax.broadcasted_iota(jnp.int32, (128, 128), 0).astype(F32)
            key = key + float(k * (128 - cap))
            put = jnp.transpose(jnp.where(place == jnp.broadcast_to(key, (128, 128)), 1.0, 0.0)).astype(BF16)
            col = jnp.transpose(jnp.broadcast_to(w, (128, 128)))[:, 0:1]
            puts.append((b, put, col))

        @pl.loop(0, width // 512)
        def _(t):
            cols = pl.ds(pl.multiple_of(t * 512, 512), 512)
            o = jnp.dot(act_own[i], wd[pl.ds(pl.multiple_of(d * half, half), half), cols], preferred_element_type=F32)
            o = o + jnp.dot(
                act_recv[i], wd[pl.ds(pl.multiple_of((1 - d) * half, half), half), cols], preferred_element_type=F32
            )
            o = o.astype(BF16)
            for k, (b, put, col) in enumerate(puts):
                lo = k * (2 * cap - 128)
                s = jnp.dot(put, o[lo:lo + 128], preferred_element_type=F32)
                tok[b, :, cols] = (s * col).astype(BF16)

        pc_copy(i).start()

    def add_part(b, other, at, t):
        cols = part(t)

        @pl.loop(0, tok.shape[1] // 32)
        def _(r):
            rs = pl.ds(pl.multiple_of(r * 32, 32), 32)
            tok[b, rs, cols] = (tok[b, rs, cols].astype(F32) + other[at, rs, cols].astype(F32)).astype(BF16)

    def reduce_core(i):
        zz, xx = group(i)
        pc_copy(i).wait_recv()

        @pl.loop(0, PIECES)
        def _(t):
            add_part(block(zz, xx, c), rc, zz * 2 + xx, t)

        @pl.when(jnp.logical_and(i % 2 == 1, i > 1))
        def _():
            px_start(zz)

        @pl.when(i == GROUPS - 1)
        def _():
            px_start(z)

    def pz_up(zz, t):
        src = tok.at[block(zz, x, c), :, part(t)]
        return remote(src, rz.at[zz, :, part(t)], pz_ss.at[zz, t], pz_rs.at[zz, t], up_dev)

    def pz_down(zz, t):
        at = jnp.where(zz == z - 1, LINE, zz)
        src = tok.at[block(zz, x, c), :, part(t)]
        return remote(src, rz.at[at, :, part(t)], pz_ss.at[zz, t], pz_rs.at[at, t], down_dev)

    def send_on(zz, t):
        @pl.when(zz > z)
        def _():
            pz_up(zz, t).start()

        @pl.when(zz < z)
        def _():
            pz_down(zz, t).start()

    def rz_wait(at, t):
        ref = rz.at[at, :, part(t)]
        remote(ref, ref, pz_ss.at[0, t], pz_rs.at[at, t], c_dev).wait_recv()

    def reduce_x(zz, onward):
        @pl.loop(0, PIECES)
        def _(t):
            px_copy(zz, t).wait_recv()
            add_part(block(zz, x, c), rx, zz, t)

            if onward:
                @pl.when(jnp.logical_not(mid))
                def _():
                    send_on(zz, t)

    @pl.loop(0, GROUPS + 4)
    def _(i):
        @pl.when(jnp.logical_and(i < GROUPS, i % 2 == 0))
        def _():
            @pl.when(jnp.logical_and(i > 0, jnp.logical_not(jnp.logical_and(mid, i == 4))))
            def _():
                take_column(order(i // 2))

            @pl.when(jnp.logical_and(mid, i == 2))
            def _():
                take_column(order(2))

        @pl.when(jnp.logical_and(i >= 2, i < GROUPS + 2))
        def _():
            down(i - 2)

        @pl.when(jnp.logical_and(i >= 3, i < GROUPS + 3))
        def _():
            reduce_core(i - 3)

        @pl.when(jnp.logical_and(i >= 1, i < GROUPS + 1))
        def _():
            activate(i - 1)

        @pl.when(i < GROUPS)
        def _():
            zz, xx = group(i)

            @pl.when(i % 2 == 1)
            def _():
                x_copy(zz, xx).wait_recv()
                c_copy(zz, xx, c).start()

            c_copy(zz, xx, 1 - c).wait_recv()
            gate_up(i)

        @pl.when(jnp.logical_and(i >= 7, i % 2 == 1))
        def _():
            reduce_x(order((i - 5) // 2), True)

    @pl.when(mid)
    def _():
        @pl.loop(0, 3 * PIECES)
        def _(kt):
            k, t = kt // PIECES, kt % PIECES
            zz = order(jnp.where(k == 2, 1, k + 2))
            rz_wait(zz, t)
            add_part(block(zz, x, c), rz, zz, t)
            send_on(zz, t)

    reduce_x(z, False)

    @pl.loop(0, PIECES)
    def _(t):
        @pl.when(z > 0)
        def _():
            rz_wait(z, t)

        @pl.when(z < LINE - 1)
        def _():
            rz_wait(LINE, t)

        cols = part(t)

        @pl.loop(0, tok.shape[1] // 32)
        def _(r):
            rs = pl.ds(pl.multiple_of(r * 32, 32), 32)
            own = tok[e, rs, cols].astype(F32)
            below = jnp.where(z > 0, rz[z, rs, cols].astype(F32), 0.0)
            above = jnp.where(z < LINE - 1, rz[LINE, rs, cols].astype(F32), 0.0)
            out_ref[rs, cols] = (own + below + above).astype(BF16)

    @pl.loop(1, experts)
    def _(k):
        meta_copy(e, (e + k) % experts).wait_send()

    gu_copy(GROUPS - 2).wait_send()
    gu_copy(GROUPS - 1).wait_send()

    @pl.loop(0, GROUPS)
    def _(i):
        act_copy(i).wait_send()
        pc_copy(i).wait_send()

    @pl.loop(0, LINE * PIECES)
    def _(zt):
        zz, t = zt // PIECES, zt % PIECES
        px_copy(zz, t).wait_send()

        @pl.when(zz > z)
        def _():
            pz_up(zz, t).wait_send()

        @pl.when(zz < z)
        def _():
            pz_down(zz, t).wait_send()


def fused(tokens, route_ids, route_weights, swap_flags, gate_weight, up_weight, down_weight):
    experts = lax.axis_size("expert")
    tok_rows, width = tokens.shape
    hidden = gate_weight.shape[2]
    cap = 5 * tok_rows * route_ids.shape[1] // (4 * experts)
    slots = jnp.arange(experts, dtype=jnp.int32)
    source = jnp.where(swap_flags == 1, (slots + experts // 2) % experts, slots)
    hit = route_ids[None, :, :] == source[:, None, None]
    served = jnp.sum(jnp.where(hit, route_weights[None], 0.0), axis=2)
    block = (tok_rows, width)
    dma = pltpu.SemaphoreType.DMA
    return pl.pallas_call(
        functools.partial(fused_kernel, cap),
        out_shape=jax.ShapeDtypeStruct(block, BF16),
        in_specs=[pl.BlockSpec(memory_space=pl.ANY)] * 5,
        out_specs=pl.BlockSpec(memory_space=pltpu.VMEM),
        scratch_shapes=[
            pltpu.VMEM((experts,) + block, BF16),
            pltpu.VMEM((width, 2 * hidden), BF16),
            pltpu.VMEM((hidden, width), BF16),
            pltpu.VMEM((2 * cap, width), BF16),
            pltpu.VMEM((experts, experts, tok_rows), F32),
            pltpu.VMEM((2, 2 * cap, hidden), BF16),
            pltpu.VMEM((2, 2 * cap, hidden), BF16),
            pltpu.VMEM((GROUPS, 2 * cap, hidden), BF16),
            pltpu.VMEM((GROUPS, 2 * cap, hidden // 2), BF16),
            pltpu.VMEM((GROUPS, 2 * cap, hidden // 2), BF16),
            pltpu.VMEM((GROUPS,) + block, BF16),
            pltpu.VMEM((LINE,) + block, BF16),
            pltpu.VMEM((LINE + 1,) + block, BF16),
            dma((5,)), dma((experts,)), dma((experts,)),
            dma((LINE,)), dma((LINE,)), dma((LINE,)), dma((LINE,)), dma((LINE,)), dma((GROUPS,)), dma((GROUPS,)),
            dma((GROUPS,)), dma((GROUPS,)), dma((GROUPS,)), dma((GROUPS,)),
            dma((GROUPS,)), dma((GROUPS,)), dma((LINE, PIECES)), dma((LINE, PIECES)),
            dma((LINE, PIECES)), dma((LINE + 1, PIECES)),
        ],
        compiler_params=pltpu.CompilerParams(
            collective_id=0, has_side_effects=True, vmem_limit_bytes=VMEM_BYTES
        ),
    )(served, tokens, gate_weight[0], up_weight[0], down_weight[0])


def per_device(tokens, route_ids, route_weights, swap_flags, gate_weight, up_weight, down_weight):
    experts = lax.axis_size("expert")
    tok_rows, quarter = tokens.shape
    choices_per = route_ids.shape[1]
    hidden = gate_weight.shape[2]
    capacity = max(2, min(tok_rows, 5 * tok_rows * choices_per // (4 * experts)))
    me = lax.axis_index("expert")
    my_slot = jnp.where(swap_flags[me] == 1, (me + experts // 2) % experts, me)

    slots = jnp.arange(experts, dtype=jnp.int32)
    dense = jnp.sum(
        jnp.where(route_ids[:, :, None] == slots[None, None, :], route_weights[:, :, None], 0.0), axis=1
    )
    all_dense = lax.all_gather(dense, "expert", axis=0, tiled=False)
    all_tokens = lax.all_gather(tokens, "expert", axis=0, tiled=False)
    mine = jnp.sum(jnp.where(slots[None, None, :] == my_slot, all_dense, 0.0), axis=2)
    chosen = mine > 0.0
    rank = jnp.cumsum(chosen.astype(jnp.int32), axis=1) - 1
    places = jnp.arange(capacity, dtype=jnp.int32)
    pick = ((rank[:, None, :] == places[None, :, None]) & chosen[:, None, :]).astype(jnp.bfloat16)

    rows = jnp.einsum("bct,btd->bcd", pick, all_tokens, preferred_element_type=jnp.bfloat16)
    rows = rows.reshape(experts * capacity, quarter)
    gate_term = jnp.dot(rows, gate_weight[0], preferred_element_type=jnp.float32)
    up_term = jnp.dot(rows, up_weight[0], preferred_element_type=jnp.float32)
    summed = lax.psum_scatter(
        jnp.concatenate([gate_term, up_term], axis=1).astype(jnp.bfloat16),
        "dp",
        scatter_dimension=0,
        tiled=True,
    ).astype(jnp.float32)
    activated = (jax.nn.silu(summed[:, :hidden]) * summed[:, hidden:]).astype(jnp.bfloat16)
    results = jnp.dot(
        lax.all_gather(activated, "dp", axis=0, tiled=True),
        down_weight[0],
        preferred_element_type=jnp.float32,
    ).astype(jnp.bfloat16)
    results = results.reshape(experts, capacity, quarter)
    spread = jnp.einsum("bct,bcd->btd", pick, results, preferred_element_type=jnp.float32)
    weighted = (mine[:, :, None] * spread).astype(jnp.bfloat16)
    return lax.psum_scatter(weighted, "expert", scatter_dimension=0, tiled=False)


def solution(mesh):
    fits = mesh.shape["expert"] == 4 * LINE and mesh.shape["dp"] == 2
    in_specs = (
        P("expert", "dp"),
        P("expert", None),
        P("expert", None),
        P(),
        P("expert", "dp", None),
        P("expert", "dp", None),
        P("expert", None, "dp"),
    )
    out_specs = P("expert", "dp")
    return jax.shard_map(
        fused if fits else per_device, mesh=mesh, in_specs=in_specs, out_specs=out_specs, check_vma=False
    )
```

```python
import functools

import jax
import jax.numpy as jnp
from jax import lax
from jax.experimental import pallas as pl
from jax.experimental.pallas import tpu as pltpu
from jax.sharding import PartitionSpec as P

BF16 = jnp.bfloat16
F32 = jnp.float32
LINE = 4
PIECES = 4
GROUPS = 8
VMEM_BYTES = 63 * 1024 * 1024


def fused_kernel(
    cap, served_ref, tokens_ref, gate_ref, up_ref, down_ref, out_ref,
    tok, wgu, wd, rows, dense, picks, puts, wcol, gu_send, gu_own, gu_recv, act_own, act_recv, rc, rx, rz,
    load_sem, meta_ss, meta_rs,
    zu_ss, zd_ss, z_rs, x_ss, x_rs, c_ss, c_rs,
    g_ss, g_rs, a_ss, a_rs,
    pc_ss, pc_rs, px_ss, px_rs, pz_ss, pz_rs,
):
    d = lax.axis_index("dp")
    e = lax.axis_index("expert")
    experts = LINE * 4
    width = tok.shape[2]
    hidden = wd.shape[0]
    half = hidden // 2
    z = e // 4
    x = (e // 2) % 2
    c = e % 2
    up_dev, down_dev = e + 4, e - 4
    x_dev = z * 4 + (1 - x) * 2 + c
    c_dev = z * 4 + x * 2 + (1 - c)
    low = z < 2
    m = jnp.where(low, z, LINE - 1 - z)
    mid = m == 1

    def order(i):
        o = jnp.where(i == 0, m, jnp.where(i - 1 < m, i - 1, i))
        return jnp.where(low, o, LINE - 1 - o)

    def group(i):
        zz = order(i // 2)
        xx = jnp.where(i % 2 == 0, x, 1 - x)
        return zz, xx

    def block(zz, xx, cc):
        return zz * 4 + xx * 2 + cc

    def remote(src, dst, ss, rs, dev):
        return pltpu.make_async_remote_copy(
            src_ref=src, dst_ref=dst, send_sem=ss, recv_sem=rs,
            device_id=(d, dev), device_id_type=pl.DeviceIdType.MESH,
        )

    def to_partner(src, dst, ss, rs):
        return pltpu.make_async_remote_copy(
            src_ref=src, dst_ref=dst, send_sem=ss, recv_sem=rs,
            device_id=(1 - d, e), device_id_type=pl.DeviceIdType.MESH,
        )

    loads = [
        pltpu.make_async_copy(tokens_ref, tok.at[e], load_sem.at[0]),
        pltpu.make_async_copy(gate_ref, wgu.at[:, pl.ds(0, hidden)], load_sem.at[1]),
        pltpu.make_async_copy(up_ref, wgu.at[:, pl.ds(hidden, hidden)], load_sem.at[2]),
        pltpu.make_async_copy(down_ref, wd, load_sem.at[3]),
        pltpu.make_async_copy(served_ref, dense.at[e], load_sem.at[4]),
    ]
    for load in loads:
        load.start()

    barrier = pltpu.get_barrier_semaphore()

    @pl.loop(1, experts)
    def _(k):
        pl.semaphore_signal(
            barrier, inc=1, device_id=(d, (e + k) % experts), device_id_type=pl.DeviceIdType.MESH
        )

    pl.semaphore_signal(barrier, inc=1, device_id=(1 - d, e), device_id_type=pl.DeviceIdType.MESH)
    pl.semaphore_wait(barrier, experts)

    def z_up(zz):
        b = tok.at[block(zz, x, c)]
        return remote(b, b, zu_ss.at[zz], z_rs.at[zz], up_dev)

    def z_down(zz):
        b = tok.at[block(zz, x, c)]
        return remote(b, b, zd_ss.at[zz], z_rs.at[zz], down_dev)

    def x_copy(zz, xx):
        b = tok.at[block(zz, xx, c)]
        return remote(b, b, x_ss.at[zz], x_rs.at[zz], x_dev)

    def c_copy(zz, xx, cc):
        b = tok.at[block(zz, xx, cc)]
        return remote(b, b, c_ss.at[zz * 2 + xx], c_rs.at[zz * 2 + xx], c_dev)

    def sends_up(zz):
        return jnp.logical_and(zz <= z, z < LINE - 1)

    def sends_down(zz):
        return jnp.logical_and(zz >= z, z > 0)

    def spread_column(zz):
        @pl.when(sends_up(zz))
        def _():
            z_up(zz).start()

        @pl.when(sends_down(zz))
        def _():
            z_down(zz).start()

        x_copy(zz, x).start()
        c_copy(zz, x, c).start()

    def take_column(zz):
        b = tok.at[block(zz, x, c)]
        remote(b, b, zu_ss.at[zz], z_rs.at[zz], c_dev).wait_recv()
        spread_column(zz)

    loads[0].wait()
    spread_column(z)
    loads[4].wait()

    def meta_copy(src, dst_dev):
        return remote(dense.at[src], dense.at[src], meta_ss.at[dst_dev], meta_rs.at[src], dst_dev)

    @pl.loop(1, experts)
    def _(k):
        meta_copy(e, (e + k) % experts).start()

    @pl.loop(1, experts)
    def _(k):
        meta_copy((e + k) % experts, (e + k) % experts).wait_recv()

    for load in loads[1:4]:
        load.wait()

    tri = jnp.where(
        lax.broadcasted_iota(jnp.int32, (128, 128), 0) <= lax.broadcasted_iota(jnp.int32, (128, 128), 1), 1.0, 0.0
    ).astype(BF16)

    @pl.loop(0, experts)
    def _(b):
        w = dense[b, pl.ds(e, 1), :]
        chosen = w > 0.0
        ones = jnp.broadcast_to(jnp.where(chosen, 1.0, 0.0), (16, 128)).astype(BF16)
        rank = jnp.dot(ones, tri, preferred_element_type=F32)[0:1]
        key = jnp.where(chosen, rank - 1.0, -1000.0)
        place = lax.broadcasted_iota(jnp.int32, (cap, 128), 0).astype(F32)
        picks[b] = jnp.where(place == jnp.broadcast_to(key, (cap, 128)), 1.0, 0.0).astype(BF16)
        key = key + jnp.where(b % 2 == c, 0.0, float(128 - cap))
        place = lax.broadcasted_iota(jnp.int32, (128, 128), 0).astype(F32)
        puts[b] = jnp.transpose(jnp.where(place == jnp.broadcast_to(key, (128, 128)), 1.0, 0.0)).astype(BF16)
        wcol[b] = jnp.transpose(jnp.broadcast_to(w, (128, 128)))

    def gate_up(i):
        zz, xx = group(i)
        for k in range(2):
            b = block(zz, xx, c if k == 0 else 1 - c)

            @pl.loop(0, width // 512, unroll=True)
            def _(t):
                cols = pl.ds(t * 512, 512)
                rows[pl.ds(k * cap, cap), cols] = jnp.dot(
                    picks[b], tok[b, :, cols], preferred_element_type=F32
                ).astype(BF16)

        slot = i % 2

        @pl.when(i >= 2)
        def _():
            gu_copy(i - 2).wait_send()

        def tile(t, which):
            at = pl.multiple_of((t // 2) * hidden + which * half + (t % 2) * 256, 256)
            return jnp.dot(rows[...], wgu[:, pl.ds(at, 256)], preferred_element_type=F32).astype(BF16)

        @pl.loop(0, 4, unroll=True)
        def _(t):
            gu_send[slot, :, pl.ds(pl.multiple_of(t * 256, 256), 256)] = tile(t, 1 - d)

        gu_copy(i).start()

        @pl.loop(0, 4, unroll=True)
        def _(t):
            gu_own[slot, :, pl.ds(pl.multiple_of(t * 256, 256), 256)] = tile(t, d)

    def gu_copy(i):
        return to_partner(gu_send.at[i % 2], gu_recv.at[i], g_ss.at[i], g_rs.at[i])

    def act_copy(i):
        return to_partner(act_own.at[i], act_recv.at[i], a_ss.at[i], a_rs.at[i])

    def activate(i):
        gu_copy(i).wait_recv()
        slot = i % 2

        @pl.loop(0, half // 128, unroll=True)
        def _(t):
            cg = pl.ds(pl.multiple_of(t * 128, 128), 128)
            cu = pl.ds(pl.multiple_of(half + t * 128, 128), 128)
            g = gu_own[slot, :, cg].astype(F32) + gu_recv[i, :, cg].astype(F32)
            u = gu_own[slot, :, cu].astype(F32) + gu_recv[i, :, cu].astype(F32)
            act_own[i, :, cg] = (g / (1.0 + jnp.exp(-g)) * u).astype(BF16)

        act_copy(i).start()

    def pc_copy(i):
        zz, xx = group(i)
        at = zz * 2 + xx
        return remote(tok.at[block(zz, xx, 1 - c)], rc.at[at], pc_ss.at[at], pc_rs.at[at], c_dev)

    piece = width // PIECES

    def part(t):
        return pl.ds(pl.multiple_of(t * piece, 128), piece)

    def px_copy(zz, t):
        return remote(
            tok.at[block(zz, 1 - x, c), :, part(t)], rx.at[zz, :, part(t)], px_ss.at[zz, t], px_rs.at[zz, t], x_dev
        )

    def px_start(zz):
        @pl.loop(0, PIECES)
        def _(t):
            px_copy(zz, t).start()

    def down(i):
        zz, xx = group(i)
        act_copy(i).wait_recv()
        c_copy(zz, xx, c).wait_send()

        @pl.when(i % 2 == 0)
        def _():
            x_copy(zz, x).wait_send()

            @pl.when(sends_up(zz))
            def _():
                z_up(zz).wait_send()

            @pl.when(sends_down(zz))
            def _():
                z_down(zz).wait_send()

        @pl.loop(0, width // 512, unroll=True)
        def _(t):
            cols = pl.ds(t * 512, 512)
            o = jnp.dot(act_own[i], wd[pl.ds(pl.multiple_of(d * half, half), half), cols], preferred_element_type=F32)
            o = o + jnp.dot(
                act_recv[i], wd[pl.ds(pl.multiple_of((1 - d) * half, half), half), cols], preferred_element_type=F32
            )
            o = o.astype(BF16)
            for k in range(2):
                b = block(zz, xx, c if k == 0 else 1 - c)
                lo = k * (2 * cap - 128)
                s = jnp.dot(puts[b], o[lo:lo + 128], preferred_element_type=F32)
                tok[b, :, cols] = (s * wcol[b, :, 0:1]).astype(BF16)

        pc_copy(i).start()

    def add_part(b, other, at, t):
        cols = part(t)

        @pl.loop(0, tok.shape[1] // 32, unroll=True)
        def _(r):
            rs = pl.ds(pl.multiple_of(r * 32, 32), 32)
            tok[b, rs, cols] = (tok[b, rs, cols].astype(F32) + other[at, rs, cols].astype(F32)).astype(BF16)

    def reduce_core(i):
        zz, xx = group(i)
        pc_copy(i).wait_recv()

        @pl.loop(0, PIECES)
        def _(t):
            add_part(block(zz, xx, c), rc, zz * 2 + xx, t)

        @pl.when(jnp.logical_and(i % 2 == 1, i > 1))
        def _():
            px_start(zz)

        @pl.when(i == GROUPS - 1)
        def _():
            px_start(z)

    def pz_up(zz, t):
        src = tok.at[block(zz, x, c), :, part(t)]
        return remote(src, rz.at[zz, :, part(t)], pz_ss.at[zz, t], pz_rs.at[zz, t], up_dev)

    def pz_down(zz, t):
        at = jnp.where(zz == z - 1, LINE, zz)
        src = tok.at[block(zz, x, c), :, part(t)]
        return remote(src, rz.at[at, :, part(t)], pz_ss.at[zz, t], pz_rs.at[at, t], down_dev)

    def send_on(zz, t):
        @pl.when(zz > z)
        def _():
            pz_up(zz, t).start()

        @pl.when(zz < z)
        def _():
            pz_down(zz, t).start()

    def rz_wait(at, t):
        ref = rz.at[at, :, part(t)]
        remote(ref, ref, pz_ss.at[0, t], pz_rs.at[at, t], c_dev).wait_recv()

    def reduce_x(zz, onward):
        @pl.loop(0, PIECES)
        def _(t):
            px_copy(zz, t).wait_recv()
            add_part(block(zz, x, c), rx, zz, t)

            if onward:
                @pl.when(jnp.logical_not(mid))
                def _():
                    send_on(zz, t)

    @pl.loop(0, GROUPS + 3)
    def _(i):
        @pl.when(jnp.logical_and(i < GROUPS, i % 2 == 0))
        def _():
            @pl.when(jnp.logical_and(i > 0, jnp.logical_not(jnp.logical_and(mid, i == 4))))
            def _():
                take_column(order(i // 2))

            @pl.when(jnp.logical_and(mid, i == 2))
            def _():
                take_column(order(2))

        @pl.when(jnp.logical_and(i >= 2, i < GROUPS + 2))
        def _():
            down(i - 2)

        @pl.when(jnp.logical_and(i >= 3, i < GROUPS + 3))
        def _():
            reduce_core(i - 3)

        @pl.when(jnp.logical_and(i >= 1, i < GROUPS + 1))
        def _():
            activate(i - 1)

        @pl.when(i < GROUPS)
        def _():
            zz, xx = group(i)

            @pl.when(i % 2 == 1)
            def _():
                x_copy(zz, xx).wait_recv()
                c_copy(zz, xx, c).start()

            c_copy(zz, xx, 1 - c).wait_recv()
            gate_up(i)

        @pl.when(i == GROUPS + 1)
        def _():
            reduce_x(order(1), True)

    @pl.loop(2, LINE)
    def _(zi):
        reduce_x(order(zi), True)

    @pl.when(mid)
    def _():
        @pl.loop(0, 3 * PIECES)
        def _(kt):
            k, t = kt // PIECES, kt % PIECES
            zz = order(jnp.where(k == 2, 1, k + 2))
            rz_wait(zz, t)
            add_part(block(zz, x, c), rz, zz, t)
            send_on(zz, t)

    reduce_x(z, False)

    @pl.loop(0, PIECES)
    def _(t):
        @pl.when(z > 0)
        def _():
            rz_wait(z, t)

        @pl.when(z < LINE - 1)
        def _():
            rz_wait(LINE, t)

        cols = part(t)

        @pl.loop(0, tok.shape[1] // 32, unroll=True)
        def _(r):
            rs = pl.ds(pl.multiple_of(r * 32, 32), 32)
            own = tok[e, rs, cols].astype(F32)
            below = jnp.where(z > 0, rz[z, rs, cols].astype(F32), 0.0)
            above = jnp.where(z < LINE - 1, rz[LINE, rs, cols].astype(F32), 0.0)
            out_ref[rs, cols] = (own + below + above).astype(BF16)

    @pl.loop(1, experts)
    def _(k):
        meta_copy(e, (e + k) % experts).wait_send()

    gu_copy(GROUPS - 2).wait_send()
    gu_copy(GROUPS - 1).wait_send()

    @pl.loop(0, GROUPS)
    def _(i):
        act_copy(i).wait_send()
        pc_copy(i).wait_send()

    @pl.loop(0, LINE * PIECES)
    def _(zt):
        zz, t = zt // PIECES, zt % PIECES
        px_copy(zz, t).wait_send()

        @pl.when(zz > z)
        def _():
            pz_up(zz, t).wait_send()

        @pl.when(zz < z)
        def _():
            pz_down(zz, t).wait_send()


def fused(tokens, route_ids, route_weights, swap_flags, gate_weight, up_weight, down_weight):
    experts = lax.axis_size("expert")
    tok_rows, width = tokens.shape
    hidden = gate_weight.shape[2]
    cap = 5 * tok_rows * route_ids.shape[1] // (4 * experts)
    slots = jnp.arange(experts, dtype=jnp.int32)
    source = jnp.where(swap_flags == 1, (slots + experts // 2) % experts, slots)
    hit = route_ids[None, :, :] == source[:, None, None]
    served = jnp.sum(jnp.where(hit, route_weights[None], 0.0), axis=2)
    block = (tok_rows, width)
    dma = pltpu.SemaphoreType.DMA
    return pl.pallas_call(
        functools.partial(fused_kernel, cap),
        out_shape=jax.ShapeDtypeStruct(block, BF16),
        in_specs=[pl.BlockSpec(memory_space=pl.ANY)] * 5,
        out_specs=pl.BlockSpec(memory_space=pltpu.VMEM),
        scratch_shapes=[
            pltpu.VMEM((experts,) + block, BF16),
            pltpu.VMEM((width, 2 * hidden), BF16),
            pltpu.VMEM((hidden, width), BF16),
            pltpu.VMEM((2 * cap, width), BF16),
            pltpu.VMEM((experts, experts, tok_rows), F32),
            pltpu.VMEM((experts, cap, tok_rows), BF16),
            pltpu.VMEM((experts, tok_rows, tok_rows), BF16),
            pltpu.VMEM((experts, tok_rows, tok_rows), F32),
            pltpu.VMEM((2, 2 * cap, hidden), BF16),
            pltpu.VMEM((2, 2 * cap, hidden), BF16),
            pltpu.VMEM((GROUPS, 2 * cap, hidden), BF16),
            pltpu.VMEM((GROUPS, 2 * cap, hidden // 2), BF16),
            pltpu.VMEM((GROUPS, 2 * cap, hidden // 2), BF16),
            pltpu.VMEM((GROUPS,) + block, BF16),
            pltpu.VMEM((LINE,) + block, BF16),
            pltpu.VMEM((LINE + 1,) + block, BF16),
            dma((5,)), dma((experts,)), dma((experts,)),
            dma((LINE,)), dma((LINE,)), dma((LINE,)), dma((LINE,)), dma((LINE,)), dma((GROUPS,)), dma((GROUPS,)),
            dma((GROUPS,)), dma((GROUPS,)), dma((GROUPS,)), dma((GROUPS,)),
            dma((GROUPS,)), dma((GROUPS,)), dma((LINE, PIECES)), dma((LINE, PIECES)),
            dma((LINE, PIECES)), dma((LINE + 1, PIECES)),
        ],
        compiler_params=pltpu.CompilerParams(
            collective_id=0, has_side_effects=True, vmem_limit_bytes=VMEM_BYTES
        ),
    )(served, tokens, gate_weight[0], up_weight[0], down_weight[0])


def per_device(tokens, route_ids, route_weights, swap_flags, gate_weight, up_weight, down_weight):
    experts = lax.axis_size("expert")
    tok_rows, quarter = tokens.shape
    choices_per = route_ids.shape[1]
    hidden = gate_weight.shape[2]
    capacity = max(2, min(tok_rows, 5 * tok_rows * choices_per // (4 * experts)))
    me = lax.axis_index("expert")
    my_slot = jnp.where(swap_flags[me] == 1, (me + experts // 2) % experts, me)

    slots = jnp.arange(experts, dtype=jnp.int32)
    dense = jnp.sum(
        jnp.where(route_ids[:, :, None] == slots[None, None, :], route_weights[:, :, None], 0.0), axis=1
    )
    all_dense = lax.all_gather(dense, "expert", axis=0, tiled=False)
    all_tokens = lax.all_gather(tokens, "expert", axis=0, tiled=False)
    mine = jnp.sum(jnp.where(slots[None, None, :] == my_slot, all_dense, 0.0), axis=2)
    chosen = mine > 0.0
    rank = jnp.cumsum(chosen.astype(jnp.int32), axis=1) - 1
    places = jnp.arange(capacity, dtype=jnp.int32)
    pick = ((rank[:, None, :] == places[None, :, None]) & chosen[:, None, :]).astype(jnp.bfloat16)

    rows = jnp.einsum("bct,btd->bcd", pick, all_tokens, preferred_element_type=jnp.bfloat16)
    rows = rows.reshape(experts * capacity, quarter)
    gate_term = jnp.dot(rows, gate_weight[0], preferred_element_type=jnp.float32)
    up_term = jnp.dot(rows, up_weight[0], preferred_element_type=jnp.float32)
    summed = lax.psum_scatter(
        jnp.concatenate([gate_term, up_term], axis=1).astype(jnp.bfloat16),
        "dp",
        scatter_dimension=0,
        tiled=True,
    ).astype(jnp.float32)
    activated = (jax.nn.silu(summed[:, :hidden]) * summed[:, hidden:]).astype(jnp.bfloat16)
    results = jnp.dot(
        lax.all_gather(activated, "dp", axis=0, tiled=True),
        down_weight[0],
        preferred_element_type=jnp.float32,
    ).astype(jnp.bfloat16)
    results = results.reshape(experts, capacity, quarter)
    spread = jnp.einsum("bct,bcd->btd", pick, results, preferred_element_type=jnp.float32)
    weighted = (mine[:, :, None] * spread).astype(jnp.bfloat16)
    return lax.psum_scatter(weighted, "expert", scatter_dimension=0, tiled=False)


def solution(mesh):
    fits = mesh.shape["expert"] == 4 * LINE and mesh.shape["dp"] == 2
    in_specs = (
        P("expert", "dp"),
        P("expert", None),
        P("expert", None),
        P(),
        P("expert", "dp", None),
        P("expert", "dp", None),
        P("expert", None, "dp"),
    )
    out_specs = P("expert", "dp")
    return jax.shard_map(
        fused if fits else per_device, mesh=mesh, in_specs=in_specs, out_specs=out_specs, check_vma=False
    )
```

```python
import functools

import jax
import jax.numpy as jnp
from jax import lax
from jax.experimental import pallas as pl
from jax.experimental.pallas import tpu as pltpu
from jax.sharding import PartitionSpec as P

BF16 = jnp.bfloat16
F32 = jnp.float32
LINE = 4
PIECES = 4
GROUPS = 8
VMEM_BYTES = 63 * 1024 * 1024


def fused_kernel(
    cap, served_ref, tokens_ref, gate_ref, up_ref, down_ref, out_ref,
    tok, wgu, wd, rows, dense, picks, puts, wcol, gu_send, gu_own, gu_recv, act_own, act_recv, rc, rx, rz,
    load_sem, meta_ss, meta_rs,
    zu_ss, zd_ss, z_rs, x_ss, x_rs, c_ss, c_rs,
    g_ss, g_rs, a_ss, a_rs,
    pc_ss, pc_rs, px_ss, px_rs, pz_ss, pz_rs,
):
    d = lax.axis_index("dp")
    e = lax.axis_index("expert")
    experts = LINE * 4
    width = tok.shape[2]
    hidden = wd.shape[0]
    half = hidden // 2
    z = e // 4
    x = (e // 2) % 2
    c = e % 2
    up_dev, down_dev = e + 4, e - 4
    x_dev = z * 4 + (1 - x) * 2 + c
    c_dev = z * 4 + x * 2 + (1 - c)
    low = z < 2
    m = jnp.where(low, z, LINE - 1 - z)
    mid = m == 1

    def order(i):
        o = jnp.where(i == 0, m, jnp.where(i - 1 < m, i - 1, i))
        return jnp.where(low, o, LINE - 1 - o)

    def group(i):
        zz = order(i // 2)
        xx = jnp.where(i % 2 == 0, x, 1 - x)
        return zz, xx

    def block(zz, xx, cc):
        return zz * 4 + xx * 2 + cc

    def remote(src, dst, ss, rs, dev):
        return pltpu.make_async_remote_copy(
            src_ref=src, dst_ref=dst, send_sem=ss, recv_sem=rs,
            device_id=(d, dev), device_id_type=pl.DeviceIdType.MESH,
        )

    def to_partner(src, dst, ss, rs):
        return pltpu.make_async_remote_copy(
            src_ref=src, dst_ref=dst, send_sem=ss, recv_sem=rs,
            device_id=(1 - d, e), device_id_type=pl.DeviceIdType.MESH,
        )

    loads = [
        pltpu.make_async_copy(tokens_ref, tok.at[e], load_sem.at[0]),
        pltpu.make_async_copy(gate_ref, wgu.at[:, pl.ds(0, hidden)], load_sem.at[1]),
        pltpu.make_async_copy(up_ref, wgu.at[:, pl.ds(hidden, hidden)], load_sem.at[2]),
        pltpu.make_async_copy(down_ref, wd, load_sem.at[3]),
        pltpu.make_async_copy(served_ref, dense.at[e], load_sem.at[4]),
    ]
    for load in loads:
        load.start()

    barrier = pltpu.get_barrier_semaphore()

    @pl.loop(1, experts)
    def _(k):
        pl.semaphore_signal(
            barrier, inc=1, device_id=(d, (e + k) % experts), device_id_type=pl.DeviceIdType.MESH
        )

    pl.semaphore_signal(barrier, inc=1, device_id=(1 - d, e), device_id_type=pl.DeviceIdType.MESH)
    pl.semaphore_wait(barrier, experts)

    def z_up(zz):
        b = tok.at[block(zz, x, c)]
        return remote(b, b, zu_ss.at[zz], z_rs.at[zz], up_dev)

    def z_down(zz):
        b = tok.at[block(zz, x, c)]
        return remote(b, b, zd_ss.at[zz], z_rs.at[zz], down_dev)

    def x_copy(zz, xx):
        b = tok.at[block(zz, xx, c)]
        return remote(b, b, x_ss.at[zz], x_rs.at[zz], x_dev)

    def c_copy(zz, xx, cc):
        b = tok.at[block(zz, xx, cc)]
        return remote(b, b, c_ss.at[zz * 2 + xx], c_rs.at[zz * 2 + xx], c_dev)

    def sends_up(zz):
        return jnp.logical_and(zz <= z, z < LINE - 1)

    def sends_down(zz):
        return jnp.logical_and(zz >= z, z > 0)

    def spread_column(zz):
        @pl.when(sends_up(zz))
        def _():
            z_up(zz).start()

        @pl.when(sends_down(zz))
        def _():
            z_down(zz).start()

        x_copy(zz, x).start()
        c_copy(zz, x, c).start()

    def take_column(zz):
        b = tok.at[block(zz, x, c)]
        remote(b, b, zu_ss.at[zz], z_rs.at[zz], c_dev).wait_recv()
        spread_column(zz)

    loads[4].wait()

    def meta_copy(src, dst_dev):
        return remote(dense.at[src], dense.at[src], meta_ss.at[dst_dev], meta_rs.at[src], dst_dev)

    @pl.loop(1, experts)
    def _(k):
        meta_copy(e, (e + k) % experts).start()

    loads[0].wait()
    spread_column(z)

    @pl.loop(1, experts)
    def _(k):
        meta_copy((e + k) % experts, (e + k) % experts).wait_recv()

    for load in loads[1:4]:
        load.wait()

    tri = jnp.where(
        lax.broadcasted_iota(jnp.int32, (128, 128), 0) <= lax.broadcasted_iota(jnp.int32, (128, 128), 1), 1.0, 0.0
    ).astype(BF16)

    @pl.loop(0, experts)
    def _(b):
        w = dense[b, pl.ds(e, 1), :]
        chosen = w > 0.0
        ones = jnp.broadcast_to(jnp.where(chosen, 1.0, 0.0), (16, 128)).astype(BF16)
        rank = jnp.dot(ones, tri, preferred_element_type=F32)[0:1]
        key = jnp.where(chosen, rank - 1.0, -1000.0)
        place = lax.broadcasted_iota(jnp.int32, (cap, 128), 0).astype(F32)
        picks[b] = jnp.where(place == jnp.broadcast_to(key, (cap, 128)), 1.0, 0.0).astype(BF16)
        key = key + jnp.where(b % 2 == c, 0.0, float(128 - cap))
        place = lax.broadcasted_iota(jnp.int32, (128, 128), 0).astype(F32)
        puts[b] = jnp.transpose(jnp.where(place == jnp.broadcast_to(key, (128, 128)), 1.0, 0.0)).astype(BF16)
        wcol[b] = jnp.transpose(jnp.broadcast_to(w, (128, 128)))

    def gate_up(i):
        zz, xx = group(i)
        for k in range(2):
            b = block(zz, xx, c if k == 0 else 1 - c)

            @pl.loop(0, width // 512, unroll=True)
            def _(t):
                cols = pl.ds(t * 512, 512)
                rows[pl.ds(k * cap, cap), cols] = jnp.dot(
                    picks[b], tok[b, :, cols], preferred_element_type=F32
                ).astype(BF16)

        slot = i % 2

        @pl.when(i >= 2)
        def _():
            gu_copy(i - 2).wait_send()

        def tile(t, which):
            at = pl.multiple_of((t // 2) * hidden + which * half + (t % 2) * 256, 256)
            return jnp.dot(rows[...], wgu[:, pl.ds(at, 256)], preferred_element_type=F32).astype(BF16)

        @pl.loop(0, 4, unroll=True)
        def _(t):
            gu_send[slot, :, pl.ds(pl.multiple_of(t * 256, 256), 256)] = tile(t, 1 - d)

        gu_copy(i).start()

        @pl.loop(0, 4, unroll=True)
        def _(t):
            gu_own[slot, :, pl.ds(pl.multiple_of(t * 256, 256), 256)] = tile(t, d)

    def gu_copy(i):
        return to_partner(gu_send.at[i % 2], gu_recv.at[i], g_ss.at[i], g_rs.at[i])

    def act_copy(i):
        return to_partner(act_own.at[i], act_recv.at[i], a_ss.at[i], a_rs.at[i])

    def activate(i):
        gu_copy(i).wait_recv()
        slot = i % 2

        @pl.loop(0, half // 128, unroll=True)
        def _(t):
            cg = pl.ds(pl.multiple_of(t * 128, 128), 128)
            cu = pl.ds(pl.multiple_of(half + t * 128, 128), 128)
            g = gu_own[slot, :, cg].astype(F32) + gu_recv[i, :, cg].astype(F32)
            u = gu_own[slot, :, cu].astype(F32) + gu_recv[i, :, cu].astype(F32)
            act_own[i, :, cg] = (g / (1.0 + jnp.exp(-g)) * u).astype(BF16)

        act_copy(i).start()

    def pc_copy(i):
        zz, xx = group(i)
        at = zz * 2 + xx
        return remote(tok.at[block(zz, xx, 1 - c)], rc.at[at], pc_ss.at[at], pc_rs.at[at], c_dev)

    piece = width // PIECES

    def part(t):
        return pl.ds(pl.multiple_of(t * piece, 128), piece)

    def px_copy(zz, t):
        return remote(
            tok.at[block(zz, 1 - x, c), :, part(t)], rx.at[zz, :, part(t)], px_ss.at[zz, t], px_rs.at[zz, t], x_dev
        )

    def px_start(zz):
        @pl.loop(0, PIECES)
        def _(t):
            px_copy(zz, t).start()

    def down(i):
        zz, xx = group(i)
        act_copy(i).wait_recv()
        c_copy(zz, xx, c).wait_send()

        @pl.when(i % 2 == 0)
        def _():
            x_copy(zz, x).wait_send()

            @pl.when(sends_up(zz))
            def _():
                z_up(zz).wait_send()

            @pl.when(sends_down(zz))
            def _():
                z_down(zz).wait_send()

        @pl.loop(0, width // 512, unroll=True)
        def _(t):
            cols = pl.ds(t * 512, 512)
            o = jnp.dot(act_own[i], wd[pl.ds(pl.multiple_of(d * half, half), half), cols], preferred_element_type=F32)
            o = o + jnp.dot(
                act_recv[i], wd[pl.ds(pl.multiple_of((1 - d) * half, half), half), cols], preferred_element_type=F32
            )
            o = o.astype(BF16)
            for k in range(2):
                b = block(zz, xx, c if k == 0 else 1 - c)
                lo = k * (2 * cap - 128)
                s = jnp.dot(puts[b], o[lo:lo + 128], preferred_element_type=F32)
                tok[b, :, cols] = (s * wcol[b, :, 0:1]).astype(BF16)

        pc_copy(i).start()

    def add_part(b, other, at, t):
        cols = part(t)

        @pl.loop(0, tok.shape[1] // 32, unroll=True)
        def _(r):
            rs = pl.ds(pl.multiple_of(r * 32, 32), 32)
            tok[b, rs, cols] = (tok[b, rs, cols].astype(F32) + other[at, rs, cols].astype(F32)).astype(BF16)

    def reduce_core(i):
        zz, xx = group(i)
        pc_copy(i).wait_recv()

        @pl.loop(0, PIECES)
        def _(t):
            add_part(block(zz, xx, c), rc, zz * 2 + xx, t)

        @pl.when(jnp.logical_and(i % 2 == 1, i > 1))
        def _():
            px_start(zz)

        @pl.when(i == GROUPS - 1)
        def _():
            px_start(z)

    def pz_up(zz, t):
        src = tok.at[block(zz, x, c), :, part(t)]
        return remote(src, rz.at[zz, :, part(t)], pz_ss.at[zz, t], pz_rs.at[zz, t], up_dev)

    def pz_down(zz, t):
        at = jnp.where(zz == z - 1, LINE, zz)
        src = tok.at[block(zz, x, c), :, part(t)]
        return remote(src, rz.at[at, :, part(t)], pz_ss.at[zz, t], pz_rs.at[at, t], down_dev)

    def send_on(zz, t):
        @pl.when(zz > z)
        def _():
            pz_up(zz, t).start()

        @pl.when(zz < z)
        def _():
            pz_down(zz, t).start()

    def rz_wait(at, t):
        ref = rz.at[at, :, part(t)]
        remote(ref, ref, pz_ss.at[0, t], pz_rs.at[at, t], c_dev).wait_recv()

    def reduce_x(zz, onward):
        @pl.loop(0, PIECES)
        def _(t):
            px_copy(zz, t).wait_recv()
            add_part(block(zz, x, c), rx, zz, t)

            if onward:
                @pl.when(jnp.logical_not(mid))
                def _():
                    send_on(zz, t)

    @pl.loop(0, GROUPS + 3)
    def _(i):
        @pl.when(jnp.logical_and(i >= 2, i < GROUPS + 2))
        def _():
            down(i - 2)

        @pl.when(jnp.logical_and(i >= 3, i < GROUPS + 3))
        def _():
            reduce_core(i - 3)

        @pl.when(jnp.logical_and(i >= 1, i < GROUPS + 1))
        def _():
            activate(i - 1)

        @pl.when(i < GROUPS)
        def _():
            zz, xx = group(i)

            @pl.when(jnp.logical_and(i % 2 == 1, i < GROUPS - 1))
            def _():
                @pl.when(jnp.logical_not(jnp.logical_and(mid, i == 3)))
                def _():
                    take_column(order((i + 1) // 2))

                @pl.when(jnp.logical_and(mid, i == 1))
                def _():
                    take_column(order(2))

            @pl.when(i % 2 == 1)
            def _():
                x_copy(zz, xx).wait_recv()
                c_copy(zz, xx, c).start()

            c_copy(zz, xx, 1 - c).wait_recv()
            gate_up(i)

        @pl.when(i == GROUPS + 1)
        def _():
            reduce_x(order(1), True)

    @pl.loop(2, LINE)
    def _(zi):
        reduce_x(order(zi), True)

    @pl.when(mid)
    def _():
        @pl.loop(0, 3 * PIECES)
        def _(kt):
            k, t = kt // PIECES, kt % PIECES
            zz = order(jnp.where(k == 2, 1, k + 2))
            rz_wait(zz, t)
            add_part(block(zz, x, c), rz, zz, t)
            send_on(zz, t)

    reduce_x(z, False)

    @pl.loop(0, PIECES)
    def _(t):
        @pl.when(z > 0)
        def _():
            rz_wait(z, t)

        @pl.when(z < LINE - 1)
        def _():
            rz_wait(LINE, t)

        cols = part(t)

        @pl.loop(0, tok.shape[1] // 32, unroll=True)
        def _(r):
            rs = pl.ds(pl.multiple_of(r * 32, 32), 32)
            own = tok[e, rs, cols].astype(F32)
            below = jnp.where(z > 0, rz[z, rs, cols].astype(F32), 0.0)
            above = jnp.where(z < LINE - 1, rz[LINE, rs, cols].astype(F32), 0.0)
            out_ref[rs, cols] = (own + below + above).astype(BF16)

    @pl.loop(1, experts)
    def _(k):
        meta_copy(e, (e + k) % experts).wait_send()

    gu_copy(GROUPS - 2).wait_send()
    gu_copy(GROUPS - 1).wait_send()

    @pl.loop(0, GROUPS)
    def _(i):
        act_copy(i).wait_send()
        pc_copy(i).wait_send()

    @pl.loop(0, LINE * PIECES)
    def _(zt):
        zz, t = zt // PIECES, zt % PIECES
        px_copy(zz, t).wait_send()

        @pl.when(zz > z)
        def _():
            pz_up(zz, t).wait_send()

        @pl.when(zz < z)
        def _():
            pz_down(zz, t).wait_send()


def fused(tokens, route_ids, route_weights, swap_flags, gate_weight, up_weight, down_weight):
    experts = lax.axis_size("expert")
    tok_rows, width = tokens.shape
    hidden = gate_weight.shape[2]
    cap = 5 * tok_rows * route_ids.shape[1] // (4 * experts)
    slots = jnp.arange(experts, dtype=jnp.int32)
    source = jnp.where(swap_flags == 1, (slots + experts // 2) % experts, slots)
    hit = route_ids[None, :, :] == source[:, None, None]
    served = jnp.sum(jnp.where(hit, route_weights[None], 0.0), axis=2)
    block = (tok_rows, width)
    dma = pltpu.SemaphoreType.DMA
    return pl.pallas_call(
        functools.partial(fused_kernel, cap),
        out_shape=jax.ShapeDtypeStruct(block, BF16),
        in_specs=[pl.BlockSpec(memory_space=pl.ANY)] * 5,
        out_specs=pl.BlockSpec(memory_space=pltpu.VMEM),
        scratch_shapes=[
            pltpu.VMEM((experts,) + block, BF16),
            pltpu.VMEM((width, 2 * hidden), BF16),
            pltpu.VMEM((hidden, width), BF16),
            pltpu.VMEM((2 * cap, width), BF16),
            pltpu.VMEM((experts, experts, tok_rows), F32),
            pltpu.VMEM((experts, cap, tok_rows), BF16),
            pltpu.VMEM((experts, tok_rows, tok_rows), BF16),
            pltpu.VMEM((experts, tok_rows, tok_rows), F32),
            pltpu.VMEM((2, 2 * cap, hidden), BF16),
            pltpu.VMEM((2, 2 * cap, hidden), BF16),
            pltpu.VMEM((GROUPS, 2 * cap, hidden), BF16),
            pltpu.VMEM((GROUPS, 2 * cap, hidden // 2), BF16),
            pltpu.VMEM((GROUPS, 2 * cap, hidden // 2), BF16),
            pltpu.VMEM((GROUPS,) + block, BF16),
            pltpu.VMEM((LINE,) + block, BF16),
            pltpu.VMEM((LINE + 1,) + block, BF16),
            dma((5,)), dma((experts,)), dma((experts,)),
            dma((LINE,)), dma((LINE,)), dma((LINE,)), dma((LINE,)), dma((LINE,)), dma((GROUPS,)), dma((GROUPS,)),
            dma((GROUPS,)), dma((GROUPS,)), dma((GROUPS,)), dma((GROUPS,)),
            dma((GROUPS,)), dma((GROUPS,)), dma((LINE, PIECES)), dma((LINE, PIECES)),
            dma((LINE, PIECES)), dma((LINE + 1, PIECES)),
        ],
        compiler_params=pltpu.CompilerParams(
            collective_id=0, has_side_effects=True, vmem_limit_bytes=VMEM_BYTES
        ),
    )(served, tokens, gate_weight[0], up_weight[0], down_weight[0])


def per_device(tokens, route_ids, route_weights, swap_flags, gate_weight, up_weight, down_weight):
    experts = lax.axis_size("expert")
    tok_rows, quarter = tokens.shape
    choices_per = route_ids.shape[1]
    hidden = gate_weight.shape[2]
    capacity = max(2, min(tok_rows, 5 * tok_rows * choices_per // (4 * experts)))
    me = lax.axis_index("expert")
    my_slot = jnp.where(swap_flags[me] == 1, (me + experts // 2) % experts, me)

    slots = jnp.arange(experts, dtype=jnp.int32)
    dense = jnp.sum(
        jnp.where(route_ids[:, :, None] == slots[None, None, :], route_weights[:, :, None], 0.0), axis=1
    )
    all_dense = lax.all_gather(dense, "expert", axis=0, tiled=False)
    all_tokens = lax.all_gather(tokens, "expert", axis=0, tiled=False)
    mine = jnp.sum(jnp.where(slots[None, None, :] == my_slot, all_dense, 0.0), axis=2)
    chosen = mine > 0.0
    rank = jnp.cumsum(chosen.astype(jnp.int32), axis=1) - 1
    places = jnp.arange(capacity, dtype=jnp.int32)
    pick = ((rank[:, None, :] == places[None, :, None]) & chosen[:, None, :]).astype(jnp.bfloat16)

    rows = jnp.einsum("bct,btd->bcd", pick, all_tokens, preferred_element_type=jnp.bfloat16)
    rows = rows.reshape(experts * capacity, quarter)
    gate_term = jnp.dot(rows, gate_weight[0], preferred_element_type=jnp.float32)
    up_term = jnp.dot(rows, up_weight[0], preferred_element_type=jnp.float32)
    summed = lax.psum_scatter(
        jnp.concatenate([gate_term, up_term], axis=1).astype(jnp.bfloat16),
        "dp",
        scatter_dimension=0,
        tiled=True,
    ).astype(jnp.float32)
    activated = (jax.nn.silu(summed[:, :hidden]) * summed[:, hidden:]).astype(jnp.bfloat16)
    results = jnp.dot(
        lax.all_gather(activated, "dp", axis=0, tiled=True),
        down_weight[0],
        preferred_element_type=jnp.float32,
    ).astype(jnp.bfloat16)
    results = results.reshape(experts, capacity, quarter)
    spread = jnp.einsum("bct,bcd->btd", pick, results, preferred_element_type=jnp.float32)
    weighted = (mine[:, :, None] * spread).astype(jnp.bfloat16)
    return lax.psum_scatter(weighted, "expert", scatter_dimension=0, tiled=False)


def solution(mesh):
    fits = mesh.shape["expert"] == 4 * LINE and mesh.shape["dp"] == 2
    in_specs = (
        P("expert", "dp"),
        P("expert", None),
        P("expert", None),
        P(),
        P("expert", "dp", None),
        P("expert", "dp", None),
        P("expert", None, "dp"),
    )
    out_specs = P("expert", "dp")
    return jax.shard_map(
        fused if fits else per_device, mesh=mesh, in_specs=in_specs, out_specs=out_specs, check_vma=False
    )
```

```python
import functools

import jax
import jax.numpy as jnp
from jax import lax
from jax.experimental import pallas as pl
from jax.experimental.pallas import tpu as pltpu
from jax.sharding import PartitionSpec as P

BF16 = jnp.bfloat16
F32 = jnp.float32
LINE = 4
PIECES = 4
GROUPS = 8
VMEM_BYTES = 63 * 1024 * 1024


def fused_kernel(
    cap, served_ref, tokens_ref, gate_ref, up_ref, down_ref, out_ref,
    tok, wgu, wd, rows, dense, picks, puts, wcol, gu_send, gu_own, gu_recv, act_own, act_recv, rc, rx, rz,
    load_sem, meta_ss, meta_rs,
    zu_ss, zd_ss, z_rs, x_ss, x_rs, c_ss, c_rs,
    g_ss, g_rs, a_ss, a_rs,
    pc_ss, pc_rs, px_ss, px_rs, pz_ss, pz_rs,
):
    d = lax.axis_index("dp")
    e = lax.axis_index("expert")
    experts = LINE * 4
    width = tok.shape[2]
    hidden = wd.shape[0]
    half = hidden // 2
    z = e // 4
    x = (e // 2) % 2
    c = e % 2
    up_dev, down_dev = e + 4, e - 4
    x_dev = z * 4 + (1 - x) * 2 + c
    c_dev = z * 4 + x * 2 + (1 - c)
    low = z < 2
    m = jnp.where(low, z, LINE - 1 - z)
    mid = m == 1

    def order(i):
        o = jnp.where(i == 0, m, jnp.where(i - 1 < m, i - 1, i))
        return jnp.where(low, o, LINE - 1 - o)

    def group(i):
        zz = order(i // 2)
        xx = jnp.where(i % 2 == 0, x, 1 - x)
        return zz, xx

    def block(zz, xx, cc):
        return zz * 4 + xx * 2 + cc

    def remote(src, dst, ss, rs, dev):
        return pltpu.make_async_remote_copy(
            src_ref=src, dst_ref=dst, send_sem=ss, recv_sem=rs,
            device_id=(d, dev), device_id_type=pl.DeviceIdType.MESH,
        )

    def to_partner(src, dst, ss, rs):
        return pltpu.make_async_remote_copy(
            src_ref=src, dst_ref=dst, send_sem=ss, recv_sem=rs,
            device_id=(1 - d, e), device_id_type=pl.DeviceIdType.MESH,
        )

    loads = [
        pltpu.make_async_copy(tokens_ref, tok.at[e], load_sem.at[0]),
        pltpu.make_async_copy(gate_ref, wgu.at[:, pl.ds(0, hidden)], load_sem.at[1]),
        pltpu.make_async_copy(up_ref, wgu.at[:, pl.ds(hidden, hidden)], load_sem.at[2]),
        pltpu.make_async_copy(down_ref, wd, load_sem.at[3]),
        pltpu.make_async_copy(served_ref, dense.at[e], load_sem.at[4]),
    ]
    for load in loads:
        load.start()

    barrier = pltpu.get_barrier_semaphore()

    @pl.loop(1, experts)
    def _(k):
        pl.semaphore_signal(
            barrier, inc=1, device_id=(d, (e + k) % experts), device_id_type=pl.DeviceIdType.MESH
        )

    pl.semaphore_signal(barrier, inc=1, device_id=(1 - d, e), device_id_type=pl.DeviceIdType.MESH)
    pl.semaphore_wait(barrier, experts)

    def z_up(zz):
        b = tok.at[block(zz, x, c)]
        return remote(b, b, zu_ss.at[zz], z_rs.at[zz], up_dev)

    def z_down(zz):
        b = tok.at[block(zz, x, c)]
        return remote(b, b, zd_ss.at[zz], z_rs.at[zz], down_dev)

    def x_copy(zz, xx):
        b = tok.at[block(zz, xx, c)]
        return remote(b, b, x_ss.at[zz], x_rs.at[zz], x_dev)

    def c_copy(zz, xx, cc):
        b = tok.at[block(zz, xx, cc)]
        return remote(b, b, c_ss.at[zz * 2 + xx], c_rs.at[zz * 2 + xx], c_dev)

    def sends_up(zz):
        return jnp.logical_and(zz <= z, z < LINE - 1)

    def sends_down(zz):
        return jnp.logical_and(zz >= z, z > 0)

    def spread_column(zz):
        @pl.when(sends_up(zz))
        def _():
            z_up(zz).start()

        @pl.when(sends_down(zz))
        def _():
            z_down(zz).start()

        x_copy(zz, x).start()
        c_copy(zz, x, c).start()

    def take_column(zz):
        b = tok.at[block(zz, x, c)]
        remote(b, b, zu_ss.at[zz], z_rs.at[zz], c_dev).wait_recv()
        spread_column(zz)

    loads[4].wait()

    def meta_copy(src, dst_dev):
        return remote(dense.at[src], dense.at[src], meta_ss.at[dst_dev], meta_rs.at[src], dst_dev)

    @pl.loop(1, experts)
    def _(k):
        meta_copy(e, (e + k) % experts).start()

    loads[0].wait()
    spread_column(z)

    @pl.loop(1, experts)
    def _(k):
        meta_copy((e + k) % experts, (e + k) % experts).wait_recv()

    for load in loads[1:4]:
        load.wait()

    tri = jnp.where(
        lax.broadcasted_iota(jnp.int32, (128, 128), 0) <= lax.broadcasted_iota(jnp.int32, (128, 128), 1), 1.0, 0.0
    ).astype(BF16)

    @pl.loop(0, experts)
    def _(b):
        w = dense[b, pl.ds(e, 1), :]
        chosen = w > 0.0
        ones = jnp.broadcast_to(jnp.where(chosen, 1.0, 0.0), (16, 128)).astype(BF16)
        rank = jnp.dot(ones, tri, preferred_element_type=F32)[0:1]
        key = jnp.where(chosen, rank - 1.0, -1000.0)
        place = lax.broadcasted_iota(jnp.int32, (cap, 128), 0).astype(F32)
        picks[b] = jnp.where(place == jnp.broadcast_to(key, (cap, 128)), 1.0, 0.0).astype(BF16)
        key = key + jnp.where(b % 2 == c, 0.0, float(128 - cap))
        place = lax.broadcasted_iota(jnp.int32, (128, 128), 0).astype(F32)
        puts[b] = jnp.transpose(jnp.where(place == jnp.broadcast_to(key, (128, 128)), 1.0, 0.0)).astype(BF16)
        wcol[b] = jnp.transpose(jnp.broadcast_to(w, (128, 128)))

    def gate_up(i):
        zz, xx = group(i)
        for k in range(2):
            b = block(zz, xx, c if k == 0 else 1 - c)

            @pl.loop(0, width // 512, unroll=True)
            def _(t):
                cols = pl.ds(t * 512, 512)
                rows[pl.ds(k * cap, cap), cols] = jnp.dot(
                    picks[b], tok[b, :, cols], preferred_element_type=F32
                ).astype(BF16)

        slot = i % 2

        @pl.when(i >= 2)
        def _():
            gu_copy(i - 2).wait_send()

        def tile(t, which):
            at = pl.multiple_of((t // 2) * hidden + which * half + (t % 2) * 256, 256)
            return jnp.dot(rows[...], wgu[:, pl.ds(at, 256)], preferred_element_type=F32).astype(BF16)

        @pl.loop(0, 4, unroll=True)
        def _(t):
            gu_send[slot, :, pl.ds(pl.multiple_of(t * 256, 256), 256)] = tile(t, 1 - d)

        gu_copy(i).start()

        @pl.loop(0, 4, unroll=True)
        def _(t):
            gu_own[slot, :, pl.ds(pl.multiple_of(t * 256, 256), 256)] = tile(t, d)

    def gu_copy(i):
        return to_partner(gu_send.at[i % 2], gu_recv.at[i], g_ss.at[i], g_rs.at[i])

    def act_copy(i):
        return to_partner(act_own.at[i], act_recv.at[i], a_ss.at[i], a_rs.at[i])

    def activate(i):
        gu_copy(i).wait_recv()
        slot = i % 2

        @pl.loop(0, half // 128, unroll=True)
        def _(t):
            cg = pl.ds(pl.multiple_of(t * 128, 128), 128)
            cu = pl.ds(pl.multiple_of(half + t * 128, 128), 128)
            g = gu_own[slot, :, cg].astype(F32) + gu_recv[i, :, cg].astype(F32)
            u = gu_own[slot, :, cu].astype(F32) + gu_recv[i, :, cu].astype(F32)
            act_own[i, :, cg] = (g / (1.0 + jnp.exp(-g)) * u).astype(BF16)

        act_copy(i).start()

    def pc_copy(i):
        zz, xx = group(i)
        at = zz * 2 + xx
        return remote(tok.at[block(zz, xx, 1 - c)], rc.at[at], pc_ss.at[at], pc_rs.at[at], c_dev)

    piece = width // PIECES

    def part(t):
        return pl.ds(pl.multiple_of(t * piece, 128), piece)

    def px_copy(zz, t):
        return remote(
            tok.at[block(zz, 1 - x, c), :, part(t)], rx.at[zz, :, part(t)], px_ss.at[zz, t], px_rs.at[zz, t], x_dev
        )

    def px_start(zz):
        @pl.loop(0, PIECES)
        def _(t):
            px_copy(zz, t).start()

    def down(i):
        zz, xx = group(i)
        act_copy(i).wait_recv()
        c_copy(zz, xx, c).wait_send()

        @pl.when(i % 2 == 0)
        def _():
            x_copy(zz, x).wait_send()

            @pl.when(sends_up(zz))
            def _():
                z_up(zz).wait_send()

            @pl.when(sends_down(zz))
            def _():
                z_down(zz).wait_send()

        @pl.loop(0, width // 512, unroll=True)
        def _(t):
            cols = pl.ds(t * 512, 512)
            o = jnp.dot(act_own[i], wd[pl.ds(pl.multiple_of(d * half, half), half), cols], preferred_element_type=F32)
            o = o + jnp.dot(
                act_recv[i], wd[pl.ds(pl.multiple_of((1 - d) * half, half), half), cols], preferred_element_type=F32
            )
            o = o.astype(BF16)
            for k in range(2):
                b = block(zz, xx, c if k == 0 else 1 - c)
                lo = k * (2 * cap - 128)
                s = jnp.dot(puts[b], o[lo:lo + 128], preferred_element_type=F32)
                tok[b, :, cols] = (s * wcol[b, :, 0:1]).astype(BF16)

        pc_copy(i).start()

    def add_part(b, other, at, t):
        cols = part(t)

        @pl.loop(0, tok.shape[1] // 32, unroll=True)
        def _(r):
            rs = pl.ds(pl.multiple_of(r * 32, 32), 32)
            tok[b, rs, cols] = (tok[b, rs, cols].astype(F32) + other[at, rs, cols].astype(F32)).astype(BF16)

    def reduce_core(i):
        zz, xx = group(i)
        pc_copy(i).wait_recv()

        @pl.loop(0, PIECES)
        def _(t):
            add_part(block(zz, xx, c), rc, zz * 2 + xx, t)

        @pl.when(jnp.logical_and(i % 2 == 1, i > 3))
        def _():
            px_start(zz)

        @pl.when(i == GROUPS - 1)
        def _():
            px_start(z)

    def pz_up(zz, t):
        src = tok.at[block(zz, x, c), :, part(t)]
        return remote(src, rz.at[zz, :, part(t)], pz_ss.at[zz, t], pz_rs.at[zz, t], up_dev)

    def pz_down(zz, t):
        at = jnp.where(zz == z - 1, LINE, zz)
        src = tok.at[block(zz, x, c), :, part(t)]
        return remote(src, rz.at[at, :, part(t)], pz_ss.at[zz, t], pz_rs.at[at, t], down_dev)

    def send_on(zz, t):
        @pl.when(zz > z)
        def _():
            pz_up(zz, t).start()

        @pl.when(zz < z)
        def _():
            pz_down(zz, t).start()

    def rz_wait(at, t):
        ref = rz.at[at, :, part(t)]
        remote(ref, ref, pz_ss.at[0, t], pz_rs.at[at, t], c_dev).wait_recv()

    def reduce_x(zz, onward):
        @pl.loop(0, PIECES)
        def _(t):
            px_copy(zz, t).wait_recv()
            add_part(block(zz, x, c), rx, zz, t)

            if onward:
                @pl.when(jnp.logical_not(mid))
                def _():
                    send_on(zz, t)

    @pl.loop(0, GROUPS + 3)
    def _(i):
        @pl.when(jnp.logical_and(i >= 2, i < GROUPS + 2))
        def _():
            down(i - 2)

        @pl.when(jnp.logical_and(i >= 3, i < GROUPS + 3))
        def _():
            reduce_core(i - 3)

        @pl.when(jnp.logical_and(i >= 1, i < GROUPS + 1))
        def _():
            activate(i - 1)

        @pl.when(i < GROUPS)
        def _():
            zz, xx = group(i)

            @pl.when(jnp.logical_and(i % 2 == 1, i < GROUPS - 1))
            def _():
                @pl.when(jnp.logical_not(jnp.logical_and(mid, i == 3)))
                def _():
                    take_column(order((i + 1) // 2))

                @pl.when(jnp.logical_and(mid, i == 1))
                def _():
                    take_column(order(2))

            @pl.when(i % 2 == 1)
            def _():
                x_copy(zz, xx).wait_recv()
                c_copy(zz, xx, c).start()

            @pl.when(i == GROUPS - 1)
            def _():
                px_start(order(1))

            c_copy(zz, xx, 1 - c).wait_recv()
            gate_up(i)

    def chain(zz):
        @pl.loop(0, PIECES)
        def _(t):
            rz_wait(zz, t)
            add_part(block(zz, x, c), rz, zz, t)
            send_on(zz, t)

    @pl.loop(1, LINE)
    def _(zi):
        reduce_x(order(zi), True)

        @pl.when(jnp.logical_and(mid, zi > 1))
        def _():
            chain(order(zi))

    @pl.when(mid)
    def _():
        chain(order(1))

    reduce_x(z, False)

    @pl.loop(0, PIECES)
    def _(t):
        @pl.when(z > 0)
        def _():
            rz_wait(z, t)

        @pl.when(z < LINE - 1)
        def _():
            rz_wait(LINE, t)

        cols = part(t)

        @pl.loop(0, tok.shape[1] // 32, unroll=True)
        def _(r):
            rs = pl.ds(pl.multiple_of(r * 32, 32), 32)
            own = tok[e, rs, cols].astype(F32)
            below = jnp.where(z > 0, rz[z, rs, cols].astype(F32), 0.0)
            above = jnp.where(z < LINE - 1, rz[LINE, rs, cols].astype(F32), 0.0)
            out_ref[rs, cols] = (own + below + above).astype(BF16)

    @pl.loop(1, experts)
    def _(k):
        meta_copy(e, (e + k) % experts).wait_send()

    gu_copy(GROUPS - 2).wait_send()
    gu_copy(GROUPS - 1).wait_send()

    @pl.loop(0, GROUPS)
    def _(i):
        act_copy(i).wait_send()
        pc_copy(i).wait_send()

    @pl.loop(0, LINE * PIECES)
    def _(zt):
        zz, t = zt // PIECES, zt % PIECES
        px_copy(zz, t).wait_send()

        @pl.when(zz > z)
        def _():
            pz_up(zz, t).wait_send()

        @pl.when(zz < z)
        def _():
            pz_down(zz, t).wait_send()


def fused(tokens, route_ids, route_weights, swap_flags, gate_weight, up_weight, down_weight):
    experts = lax.axis_size("expert")
    tok_rows, width = tokens.shape
    hidden = gate_weight.shape[2]
    cap = 5 * tok_rows * route_ids.shape[1] // (4 * experts)
    slots = jnp.arange(experts, dtype=jnp.int32)
    source = jnp.where(swap_flags == 1, (slots + experts // 2) % experts, slots)
    hit = route_ids[None, :, :] == source[:, None, None]
    served = jnp.sum(jnp.where(hit, route_weights[None], 0.0), axis=2)
    block = (tok_rows, width)
    dma = pltpu.SemaphoreType.DMA
    return pl.pallas_call(
        functools.partial(fused_kernel, cap),
        out_shape=jax.ShapeDtypeStruct(block, BF16),
        in_specs=[pl.BlockSpec(memory_space=pl.ANY)] * 5,
        out_specs=pl.BlockSpec(memory_space=pltpu.VMEM),
        scratch_shapes=[
            pltpu.VMEM((experts,) + block, BF16),
            pltpu.VMEM((width, 2 * hidden), BF16),
            pltpu.VMEM((hidden, width), BF16),
            pltpu.VMEM((2 * cap, width), BF16),
            pltpu.VMEM((experts, experts, tok_rows), F32),
            pltpu.VMEM((experts, cap, tok_rows), BF16),
            pltpu.VMEM((experts, tok_rows, tok_rows), BF16),
            pltpu.VMEM((experts, tok_rows, tok_rows), F32),
            pltpu.VMEM((2, 2 * cap, hidden), BF16),
            pltpu.VMEM((2, 2 * cap, hidden), BF16),
            pltpu.VMEM((GROUPS, 2 * cap, hidden), BF16),
            pltpu.VMEM((GROUPS, 2 * cap, hidden // 2), BF16),
            pltpu.VMEM((GROUPS, 2 * cap, hidden // 2), BF16),
            pltpu.VMEM((GROUPS,) + block, BF16),
            pltpu.VMEM((LINE,) + block, BF16),
            pltpu.VMEM((LINE + 1,) + block, BF16),
            dma((5,)), dma((experts,)), dma((experts,)),
            dma((LINE,)), dma((LINE,)), dma((LINE,)), dma((LINE,)), dma((LINE,)), dma((GROUPS,)), dma((GROUPS,)),
            dma((GROUPS,)), dma((GROUPS,)), dma((GROUPS,)), dma((GROUPS,)),
            dma((GROUPS,)), dma((GROUPS,)), dma((LINE, PIECES)), dma((LINE, PIECES)),
            dma((LINE, PIECES)), dma((LINE + 1, PIECES)),
        ],
        compiler_params=pltpu.CompilerParams(
            collective_id=0, has_side_effects=True, vmem_limit_bytes=VMEM_BYTES
        ),
    )(served, tokens, gate_weight[0], up_weight[0], down_weight[0])


def per_device(tokens, route_ids, route_weights, swap_flags, gate_weight, up_weight, down_weight):
    experts = lax.axis_size("expert")
    tok_rows, quarter = tokens.shape
    choices_per = route_ids.shape[1]
    hidden = gate_weight.shape[2]
    capacity = max(2, min(tok_rows, 5 * tok_rows * choices_per // (4 * experts)))
    me = lax.axis_index("expert")
    my_slot = jnp.where(swap_flags[me] == 1, (me + experts // 2) % experts, me)

    slots = jnp.arange(experts, dtype=jnp.int32)
    dense = jnp.sum(
        jnp.where(route_ids[:, :, None] == slots[None, None, :], route_weights[:, :, None], 0.0), axis=1
    )
    all_dense = lax.all_gather(dense, "expert", axis=0, tiled=False)
    all_tokens = lax.all_gather(tokens, "expert", axis=0, tiled=False)
    mine = jnp.sum(jnp.where(slots[None, None, :] == my_slot, all_dense, 0.0), axis=2)
    chosen = mine > 0.0
    rank = jnp.cumsum(chosen.astype(jnp.int32), axis=1) - 1
    places = jnp.arange(capacity, dtype=jnp.int32)
    pick = ((rank[:, None, :] == places[None, :, None]) & chosen[:, None, :]).astype(jnp.bfloat16)

    rows = jnp.einsum("bct,btd->bcd", pick, all_tokens, preferred_element_type=jnp.bfloat16)
    rows = rows.reshape(experts * capacity, quarter)
    gate_term = jnp.dot(rows, gate_weight[0], preferred_element_type=jnp.float32)
    up_term = jnp.dot(rows, up_weight[0], preferred_element_type=jnp.float32)
    summed = lax.psum_scatter(
        jnp.concatenate([gate_term, up_term], axis=1).astype(jnp.bfloat16),
        "dp",
        scatter_dimension=0,
        tiled=True,
    ).astype(jnp.float32)
    activated = (jax.nn.silu(summed[:, :hidden]) * summed[:, hidden:]).astype(jnp.bfloat16)
    results = jnp.dot(
        lax.all_gather(activated, "dp", axis=0, tiled=True),
        down_weight[0],
        preferred_element_type=jnp.float32,
    ).astype(jnp.bfloat16)
    results = results.reshape(experts, capacity, quarter)
    spread = jnp.einsum("bct,bcd->btd", pick, results, preferred_element_type=jnp.float32)
    weighted = (mine[:, :, None] * spread).astype(jnp.bfloat16)
    return lax.psum_scatter(weighted, "expert", scatter_dimension=0, tiled=False)


def solution(mesh):
    fits = mesh.shape["expert"] == 4 * LINE and mesh.shape["dp"] == 2
    in_specs = (
        P("expert", "dp"),
        P("expert", None),
        P("expert", None),
        P(),
        P("expert", "dp", None),
        P("expert", "dp", None),
        P("expert", None, "dp"),
    )
    out_specs = P("expert", "dp")
    return jax.shard_map(
        fused if fits else per_device, mesh=mesh, in_specs=in_specs, out_specs=out_specs, check_vma=False
    )
```
